128 devices in a mesh: tm: 8 (over z, x_lo), space: 16 (over x_hi, y, core).
Axes of the slice: x: 4 (x_hi: 2, x_lo: 2; x = x_hi * 2 + x_lo), y: 4, z: 4, core: 2. Of those that a mesh axis runs over, the one named last changes fastest.
Arguments:
- activations: bfloat16 [1, 32, 1024, 1280], P(None, 'tm', 'space'), may hold values from -6 to 6
- grad_out: bfloat16 [1, 32, 1024, 1280], P(None, 'tm', 'space'), may hold values from -6 to 6
- norm_gain: float32 [1280], replicated, may hold values from 0.1 to 1.9
- qkv_weight: bfloat16 [1280, 3840], replicated, may hold values from -4 to 4, as said below
- out_weight: bfloat16 [1280, 1280], replicated, may hold values from -0.15625 to 0.15625
Outputs:
- grad_tokens: bfloat16 [1, 32, 1024, 1280], P(None, 'tm', 'space')
- qkv_grad: float32 [1280, 3840], P(('tm', 'space'))
- out_grad: float32 [1280, 1280], P(('tm', 'space'))
- gain_grad: float32 [1280], P(('tm', 'space'))
The draws below stay inside these ranges and needn't reach their ends.
Inputs may be any that keep to these rules, and one draw needn't show every extreme that they name: `qkv_weight`: columns ordered (query, key, value), then head, then position in the head.
All inputs are finite; a program needn't handle non-finite values.
Results may differ from the reference program's by a relative error of at most 0.015.
The reference program's roundings to bfloat16 on the way count: a program that leaves them out, or rounds other values in their place, can miss the bound.
Values may be sent and summed in bfloat16 or wider, within the bound.
No kernel may reach another device: no remote copies, remote signals or barrier semaphores. Data moves between devices by JAX's collectives and lax.ppermute only.
A program may use at most 192 MiB of HBM per device.

```python
import math
import jax
import jax.numpy as jnp
from jax import lax

D = 1280
HEADS = 16
FRAMES = 32
VIDEOS = 1
PATCHES = 1024


def draw_activations(key, part):
    key = jax.random.fold_in(key, 11)
    first = jax.random.fold_in(key, 0)
    values = jax.random.normal(first, (VIDEOS, FRAMES, PATCHES, D), jnp.float32)
    return jnp.clip(values, -6.0, 6.0).astype(jnp.bfloat16)


def draw_qkv_weight(key, part):
    key = jax.random.fold_in(key, 12)
    first = jax.random.fold_in(key, 0)
    spread = D ** (-0.5)
    values = jnp.clip(jax.random.normal(first, (D, 3 * D), jnp.float32), -6.0, 6.0) * spread
    return values.astype(jnp.bfloat16)


def block_scale(stream_key, extent, cuts, smallest, high):
    factor_of, own = 1.0, jax.random.fold_in(stream_key, 6)
    for dim, blocks in cuts:
        draws = jnp.exp(jax.random.uniform(jax.random.fold_in(own, dim), (blocks,), jnp.float32, smallest / len(cuts), high / len(cuts)))
        factor_of = factor_of * jnp.repeat(draws, extent[dim] // blocks).reshape([-1 if axis == dim else 1 for axis in range(len(extent))])
    return factor_of


def bell_draw(stream_key, extent, width, bound, cuts=(), kind=jnp.bfloat16):
    gain = block_scale(stream_key, extent, cuts, -0.22, 0.18) if cuts else 1.0
    values = jax.random.normal(stream_key, extent, jnp.float32) * width * gain
    return jnp.minimum(jnp.maximum(values, -bound), bound).astype(kind)


def setup_inputs(seed: int = 0) -> dict:
    arg_keys = jax.random.split(jax.random.key(seed), 6)
    return {
        "activations": draw_activations(jax.random.fold_in(arg_keys[5], 71), 0),
        "grad_out": bell_draw(arg_keys[1], (VIDEOS, FRAMES, PATCHES, D), 1.0, 6.0, ((1, 8), (2, 16))),
        "norm_gain": jnp.clip(1.0 + 0.18 * jax.random.normal(arg_keys[2], (D,), jnp.float32), 0.1, 1.9),
        "qkv_weight": draw_qkv_weight(jax.random.fold_in(arg_keys[5], 71), 0),
        "out_weight": bell_draw(arg_keys[4], (D, D), D ** -0.5, 0.15625),
    }


def contract(form, left, right):
    return jnp.einsum(form, left.astype(jnp.float32), right.astype(jnp.float32))

def block_terms(activations, grad_out, norm_gain, qkv_weight, out_weight):
    video_count, frame_count, place_count, model_width = activations.shape
    head_size = model_width // HEADS
    token_count = video_count * frame_count * place_count
    inverse_root = 1.0 / math.sqrt(head_size)
    x_wide = activations.astype(jnp.float32)
    row_mean = lax.optimization_barrier(jnp.mean(x_wide, axis=-1, keepdims=True))
    centred = x_wide - row_mean
    variance = lax.optimization_barrier(jnp.mean(centred * centred, axis=-1, keepdims=True))
    inv_std = lax.rsqrt(variance + 1e-06)
    normalized = centred * inv_std
    gained = (normalized * norm_gain).astype(jnp.bfloat16)
    flat_norm = gained.reshape(token_count, model_width)
    qkv_all = jnp.dot(flat_norm, qkv_weight, preferred_element_type=jnp.float32).astype(jnp.bfloat16)
    qkv_all = qkv_all.reshape(video_count, frame_count, place_count, 3, HEADS, head_size)
    query_rows = qkv_all[:, :, :, 0]
    key_rows = qkv_all[:, :, :, 1]
    value_rows = qkv_all[:, :, :, 2]
    scores = contract('vfphe,vgphe->vphfg', query_rows, key_rows) * inverse_root
    row_max = lax.optimization_barrier(jnp.max(scores, axis=-1, keepdims=True))
    shifted = jnp.exp(scores - row_max)
    attn_prob = shifted / lax.optimization_barrier(jnp.sum(shifted, axis=-1, keepdims=True))
    prob_low = attn_prob.astype(jnp.bfloat16)
    attended = contract('vphfg,vgphe->vfphe', prob_low, value_rows).astype(jnp.bfloat16)
    attended = attended.reshape(token_count, model_width)
    cotangent = grad_out.reshape(token_count, model_width)
    out_term = lax.dot_general(attended, cotangent, (((0,), (0,)), ((), ())), preferred_element_type=jnp.float32)
    attn_grad = lax.dot_general(cotangent, out_weight, (((1,), (1,)), ((), ())), preferred_element_type=jnp.float32)
    attn_grad = attn_grad.astype(jnp.bfloat16).reshape(video_count, frame_count, place_count, HEADS, head_size)
    prob_grad = contract('vfphe,vgphe->vphfg', attn_grad, value_rows)
    score_grad = (attn_prob * (prob_grad - lax.optimization_barrier(jnp.sum(prob_grad * attn_prob, axis=-1, keepdims=True))) * inverse_root).astype(jnp.bfloat16)
    value_grad = contract('vphfg,vfphe->vgphe', prob_low, attn_grad).astype(jnp.bfloat16)
    query_grad = contract('vphfg,vgphe->vfphe', score_grad, key_rows).astype(jnp.bfloat16)
    key_grad = contract('vphfg,vfphe->vgphe', score_grad, query_rows).astype(jnp.bfloat16)
    stacked = jnp.stack([query_grad, key_grad, value_grad], axis=3).reshape(token_count, 3 * model_width)
    qkv_term = lax.dot_general(flat_norm, stacked, (((0,), (0,)), ((), ())), preferred_element_type=jnp.float32)
    normed_grad = lax.dot_general(stacked, qkv_weight, (((1,), (1,)), ((), ())), preferred_element_type=jnp.float32)
    flat_hat = normalized.reshape(token_count, model_width)
    gain_term = lax.optimization_barrier(jnp.sum(normed_grad * flat_hat, axis=0))
    scaled_grad = normed_grad * norm_gain
    flat_std = inv_std.reshape(token_count, 1)
    input_grad = flat_std * (scaled_grad - lax.optimization_barrier(jnp.mean(scaled_grad, axis=-1, keepdims=True)) - flat_hat * lax.optimization_barrier(jnp.mean(scaled_grad * flat_hat, axis=-1, keepdims=True)))
    result = (cotangent.astype(jnp.float32) + input_grad).astype(jnp.bfloat16)
    return (result.reshape(video_count, frame_count, place_count, model_width), qkv_term, out_term, gain_term)

def reference(activations, grad_out, norm_gain, qkv_weight, out_weight):
    block_size = math.gcd(PATCHES, 64)
    block_count = PATCHES // block_size

    def add_block(totals, index):
        start = (index * block_size).astype(jnp.int32)
        x_block = lax.dynamic_slice_in_dim(activations, start, block_size, 2)
        cot_block = lax.dynamic_slice_in_dim(grad_out, start, block_size, 2)
        result, qkv_term, out_term, gain_term = block_terms(x_block, cot_block, norm_gain, qkv_weight, out_weight)
        return ((totals[0] + qkv_term, totals[1] + out_term, totals[2] + gain_term), result)
    initial = (jnp.zeros((D, 3 * D), jnp.float32), jnp.zeros((D, D), jnp.float32), jnp.zeros((D,), jnp.float32))
    totals, pieces = lax.scan(add_block, initial, jnp.arange(block_count, dtype=jnp.int32))
    grad_tokens = jnp.transpose(pieces, (1, 2, 0, 3, 4)).reshape(VIDEOS, FRAMES, PATCHES, D)
    factor = 1.0 / math.sqrt(VIDEOS * FRAMES * PATCHES)
    return (grad_tokens, totals[0] * factor, totals[1] * factor, totals[2] * factor)
```

```python
import functools
import math

import jax
import jax.numpy as jnp
from jax import lax
from jax.experimental import pallas as pl
from jax.experimental.pallas import tpu as pltpu
from jax.sharding import Mesh, PartitionSpec as P

D = 1280
HEADS = 16
HEAD = 80
HALF = 640
TOKENS = 256
INVERSE_ROOT = 1.0 / math.sqrt(HEAD)
FACTOR = 1.0 / math.sqrt(32 * 1024)
BF16, F32 = jnp.bfloat16, jnp.float32
ORDER_A = (("z", "y", "x"), ("y", "x", "z"))
ORDER_B = (("x", "y", "z"), ("x", "y", "z"))
WIDTH_A, WIDTH_B = 1920, 768
NN = (((1,), (0,)), ((), ()))
NT = (((1,), (1,)), ((), ()))
TN = (((0,), (0,)), ((), ()))


def dot(left, right, dims=NN):
    return lax.dot_general(left, right, dims, preferred_element_type=F32)


def call(body, outs, operands, scalars=0, flops=0, scratch=(), after=None, results=pltpu.VMEM,
         hbm=(), last=False):
    vmem = pl.BlockSpec(memory_space=pltpu.VMEM)
    smem = pl.BlockSpec(memory_space=pltpu.SMEM)
    count, tokens = len(operands), [] if last else [pltpu.VMEM((8, 128), F32)]
    size = sum(math.prod(o.shape) * o.dtype.itemsize for o in list(operands) + list(outs))
    given = list(operands) + ([] if after is None else list(after))
    spaces = [smem] * scalars + [vmem] * (len(given) - scalars)
    placed = [
        value if place < scalars else pltpu.with_memory_space_constraint(value, pltpu.VMEM)
        for place, value in enumerate(given)
    ]
    for place in hbm:
        spaces[place] = pl.BlockSpec(memory_space=pl.ANY)
        placed[place] = from_hbm(given[place])

    def run(*refs):
        results, rest = refs[len(placed):len(placed) + len(outs)], refs[len(placed) + len(outs):]
        if not last:
            rest[0][...] = jnp.zeros((8, 128), F32)
            rest = rest[1:]
        body(*refs[:count], *results, *rest)

    given = pl.pallas_call(
        run,
        out_shape=[results(o.shape, o.dtype) for o in outs] + tokens,
        in_specs=spaces,
        out_specs=[vmem] * (len(outs) + len(tokens)),
        scratch_shapes=scratch,
        compiler_params=pltpu.CompilerParams(vmem_limit_bytes=16 * 2**20),
        cost_estimate=pl.CostEstimate(
            flops=flops, bytes_accessed=size // 4 if flops else 1, transcendentals=0
        ),
    )(*placed)
    return list(given[:len(outs)]), list(given[len(outs):])


def late(value, after):
    vmem, anywhere = pl.BlockSpec(memory_space=pltpu.VMEM), pl.BlockSpec(memory_space=pl.ANY)

    def body(*refs):
        refs[-1][...] = jnp.zeros((8, 128), F32)

    value, token = pl.pallas_call(
        body,
        out_shape=[jax.ShapeDtypeStruct(value.shape, value.dtype), pltpu.VMEM((8, 128), F32)],
        in_specs=[anywhere] + [vmem] * len(after), out_specs=[anywhere, vmem],
        input_output_aliases={0: 0},
        compiler_params=pltpu.CompilerParams(vmem_limit_bytes=2**20),
        cost_estimate=pl.CostEstimate(flops=10**7, bytes_accessed=1, transcendentals=0),
    )(value, *[pltpu.with_memory_space_constraint(array, pltpu.VMEM) for array in after])
    return value, [token]


def from_hbm(value):
    return pltpu.with_memory_space_constraint(value, pltpu.HBM)


def shape(rows, columns, kind=BF16):
    return jax.ShapeDtypeStruct((rows, columns), kind)


def side(both_ref, which, columns=slice(None)):
    value = both_ref[:, 32 * which:32 * which + 32, columns]
    return value.reshape(TOKENS, value.shape[-1])


def normalize(both_ref):
    x_wide = side(both_ref, 0).astype(F32)
    centred = x_wide - jnp.mean(x_wide, axis=-1, keepdims=True)
    variance = jnp.mean(centred * centred, axis=-1, keepdims=True)
    inv_std = lax.rsqrt(variance + 1e-06)
    return centred * inv_std, inv_std


def half(place_ref, own):
    core = place_ref[3] if own else 1 - place_ref[3]
    return pl.ds(pl.multiple_of(core * HALF, 128), HALF)


def forward_body(place_ref, both_ref, gain_ref, weight_ref, gained_ref, qkv_ref, cot_ref,
                 held_ref, sems):
    pieces = [slice(step * HALF, (step + 1) * HALF) for step in range(6)]
    copies = [
        pltpu.make_async_copy(weight_ref.at[:, piece], held_ref.at[:, piece], sems.at[step])
        for step, piece in enumerate(pieces)
    ]
    for copy in copies[:2]:
        copy.start()
    normalized, _ = normalize(both_ref)
    gained = (normalized * gain_ref[...]).astype(BF16)
    gained_ref[...] = gained
    cot_ref[...] = side(both_ref, 1, half(place_ref, False))
    for step, (copy, piece) in enumerate(zip(copies, pieces)):
        copy.wait()
        if step + 2 < len(copies):
            copies[step + 2].start()
        qkv_ref[:, piece] = dot(gained, held_ref[:, piece]).astype(BF16)


def attention_body(group_ref, qkv_ref, both_ref, weight_ref, att_ref, stack_ref, ag_ref,
                   bias_ref):
    start = pl.multiple_of(group_ref[0] * HALF, 128)
    ag_ref[...] = dot(side(both_ref, 1), weight_ref[pl.ds(start, HALF), :], NT).astype(BF16)
    row = lax.broadcasted_iota(jnp.int32, (TOKENS, TOKENS), 0)
    column = lax.broadcasted_iota(jnp.int32, (TOKENS, TOKENS), 1)
    bias_ref[...] = jnp.where((row & 7) == (column & 7), 0.0, -1e30)
    tiles = [[[] for _ in range(5)] for _ in range(4)]
    for head in range(8):
        low, high = head * HEAD, (head + 1) * HEAD
        first, last = low // 128 * 128, -(-high // 128) * 128
        width = last - first
        lanes = lax.broadcasted_iota(jnp.int32, (1, width), 1) + first
        keep = jnp.where((lanes >= low) & (lanes < high), 1.0, 0.0).astype(BF16)

        def cut(part):
            return qkv_ref[:, pl.ds(pl.multiple_of(start + part * D + first, 128), width)] * keep

        query, key, value = cut(0), cut(1), cut(2)
        grad = ag_ref[:, first:last] * keep
        scores = dot(key, query, NT) + bias_ref[...]
        shifted = jnp.exp((scores - jnp.max(scores, axis=0, keepdims=True)) * INVERSE_ROOT)
        prob = shifted * (1.0 / jnp.sum(shifted, axis=0, keepdims=True))
        prob_low = prob.astype(BF16)
        prob_grad = dot(value, grad, NT)
        mixed = jnp.sum(prob_grad * prob, axis=0, keepdims=True)
        score_grad = (prob * (prob_grad - mixed) * INVERSE_ROOT).astype(BF16)
        results = (
            dot(prob_low, value, TN), dot(score_grad, key, TN), dot(score_grad, query),
            dot(prob_low, grad),
        )
        for kind, result in enumerate(results):
            for tile in range(width // 128):
                piece = result[:, tile * 128:(tile + 1) * 128]
                tiles[kind][first // 128 + tile].append(piece)
    for kind in range(4):
        for tile in range(5):
            total = sum(tiles[kind][tile][1:], tiles[kind][tile][0]).astype(BF16)
            if kind == 0:
                att_ref[:, tile * 128:(tile + 1) * 128] = total
            else:
                at = (kind - 1) * HALF + tile * 128
                stack_ref[:, at:at + 128] = total


def input_grad_body(place_ref, both_ref, gain_ref, weight_ref, mine_ref, other_ref, pick_ref,
                    grad_ref, keep, give, joined_ref):
    for own, stack_ref in ((True, mine_ref), (False, other_ref)):
        group = place_ref[3] if own else 1 - place_ref[3]
        for part in range(3):
            columns = pl.ds(pl.multiple_of(group * HALF + part * D, 128), HALF)
            joined_ref[:, columns] = stack_ref[:, part * HALF:(part + 1) * HALF]
    normed_grad = dot(joined_ref[...], weight_ref[...], NT)
    normalized, inv_std = normalize(both_ref)
    scaled = normed_grad * gain_ref[...]
    inner = scaled - jnp.mean(scaled, axis=-1, keepdims=True)
    inner -= normalized * jnp.mean(scaled * normalized, axis=-1, keepdims=True)
    grad_ref[...] = (side(both_ref, 1).astype(F32) + inv_std * inner).astype(BF16)
    gain = jnp.sum(normed_grad * normalized, axis=0, keepdims=True)
    high = gain.astype(BF16).astype(F32)
    middle = (gain - high).astype(BF16).astype(F32)
    row = lax.broadcasted_iota(jnp.int32, (16, D), 0)
    split = jnp.where(row == 2, gain - high - middle, 0.0)
    split = jnp.where(row == 0, high, jnp.where(row == 1, middle, split)).astype(BF16)
    blocks = []
    for block in range(4):
        rows = slice(block * 320, (block + 1) * 320)
        ordered = jnp.sum(dot(split, pick_ref[rows, :], NT), axis=0, keepdims=True)
        blocks.append(jnp.concatenate([ordered, jnp.zeros((1, 64), F32)], axis=1))
    even = (place_ref[1] & 1) == 0
    near = jnp.where(even, blocks[1], blocks[3])
    far = jnp.where(even, blocks[3], blocks[1])
    rest = jnp.zeros((6, 384), F32)
    keep[...] = jnp.concatenate([blocks[0], near, rest], axis=0)
    give[...] = jnp.concatenate([blocks[2], far, rest], axis=0)


def gain_body(keep, arrived, own, give):
    total = keep[...] + arrived[...]
    own[...] = total
    give[...] = jnp.concatenate([total[1:8], total[0:1]], axis=0)


def pick(source):
    lanes = lax.broadcasted_iota(jnp.int32, (source.shape[0], D), 1)
    return jnp.where(lanes == source, 1.0, 0.0).astype(BF16)


def relative_rows(place_ref, order, block):
    here = {"z": place_ref[0], "x": place_ref[1], "y": place_ref[2]}
    on_first = place_ref[3] == 0
    row = lax.broadcasted_iota(jnp.int32, (320, 1), 0)

    def count(value, size):
        return sum(jnp.where(value >= size * step, 1, 0) for step in (1, 2, 3))

    def offset(axis, at):
        if axis == "x":
            return (at & 1) * 160 + (at >> 1) * 80
        return at * (320 if axis == "z" else 20)

    second = count(row, 80)
    row = row - 80 * second
    third = count(row, 20)
    row = row - 20 * third
    for level, step in enumerate((block, second, third)):
        one, two = (
            offset(axes[level], (here[axes[level]] + step) & 3) for axes in order
        )
        row = row + jnp.where(on_first, one, two)
    return row


def ready_body(place_ref, pick_a, pick_b, pick_att, token):
    token[...] = jnp.zeros((8, 128), F32)
    for step in range(4):
        rows = slice(step * 320, (step + 1) * 320)
        pick_a[rows, :] = pick(relative_rows(place_ref, ORDER_A, step))
        feature = relative_rows(place_ref, ORDER_B, step)
        pick_b[rows, :] = pick(feature)
        feature = feature + place_ref[3] * HALF
        pick_att[rows, :] = pick(jnp.where(feature >= D, feature - D, feature))


def gained_body(pick_ref, own_ref, partner_ref, out):
    for step in range(4):
        rows = slice(step * 320, (step + 1) * 320)
        out[rows, :TOKENS] = dot(pick_ref[rows, :], own_ref[...], NT).astype(BF16)
        out[rows, TOKENS:] = dot(pick_ref[rows, :], partner_ref[...], NT).astype(BF16)


def turn_body(pick_att, mine, other, their_mine, their_other, att_out):
    sides = ((mine, other), (their_other, their_mine))
    for step in range(4):
        rows = slice(step * 320, (step + 1) * 320)
        for which, (first, second) in enumerate(sides):
            turned = dot(pick_att[rows, :HALF], first[...], NT)
            turned += dot(pick_att[rows, HALF:], second[...], NT)
            att_out[rows, which * TOKENS:(which + 1) * TOKENS] = turned.astype(BF16)


def term_a(rows, gained, stack, their_stack):
    return dot(gained[rows, :TOKENS], stack[...]) + dot(gained[rows, TOKENS:], their_stack[...])


def term_b(rows, place_ref, both, their_cot, att):
    outer = dot(att[rows, :TOKENS], side(both, 1, half(place_ref, True)))
    return outer + dot(att[rows, TOKENS:], their_cot[...])


def early_body(term, count, *refs):
    plus, minus = refs[count:]
    far = term(slice(640, 960), *refs[:count])
    plus[0:160, :] = far[0:160].astype(BF16)
    minus[0:160, :] = far[160:320].astype(BF16)
    plus[160:320, :] = term(slice(480, 640), *refs[:count]).astype(BF16)
    minus[160:320, :] = term(slice(960, 1120), *refs[:count]).astype(BF16)


def relay_body(term, count, *refs):
    from_minus, from_plus, plus, minus = refs[count:]
    up = term(slice(320, 480), *refs[:count]) + from_minus[0:160, :].astype(F32)
    down = term(slice(1120, 1280), *refs[:count]) + from_plus[0:160, :].astype(F32)
    plus[...] = up.astype(BF16)
    minus[...] = down.astype(BF16)


def own_body(term, count, *refs):
    from_minus, from_plus, own = refs[count:]
    total = term(slice(0, 320), *refs[:count])
    own[0:160, :] = total[0:160] + from_plus[160:320, :].astype(F32)
    own[160:320, :] = total[160:320] + from_minus[160:320, :].astype(F32)


def second_early_body(own, from_minus, from_plus, *refs):
    gains, (rest, plus, minus) = refs[:-3], refs[-3:]
    upper = own[0:160, :] + from_minus[...].astype(F32)
    lower = own[160:320, :] + from_plus[...].astype(F32)
    if gains:
        line = gains[0][0:1, :] + gains[1][0:1, :]
        row = lax.broadcasted_iota(jnp.int32, (320, 384), 0)
        lane = lax.broadcasted_iota(jnp.int32, (320, 384), 1)
        column = jnp.sum(jnp.where(row == lane, line, 0.0), axis=-1, keepdims=True)
        column = jnp.where(lane[:, :128] == 0, column, 0.0)
        upper = jnp.concatenate([upper, column[0:160]], axis=1)
        lower = jnp.concatenate([lower, column[160:320]], axis=1)
    rest[0:120, :] = upper[0:120]
    plus[40:80, :] = upper[120:160]
    plus[0:40, :] = lower[0:40]
    minus[0:80, :] = lower[40:120]
    rest[120:160, :] = lower[120:160]


def second_relay_body(rest, from_minus, from_plus, plus, minus, part):
    plus[...] = rest[80:120, :] + from_minus[0:40, :]
    minus[...] = rest[120:160, :] + from_plus[0:40, :]
    part[0:40, :] = rest[0:40, :] + from_plus[40:80, :]
    part[40:80, :] = rest[40:80, :] + from_minus[40:80, :]


def third_body(part, last_minus, last_plus, own, one, two, three):
    upper = part[0:40, :] + last_minus[...]
    lower = part[40:80, :] + last_plus[...]
    own[...] = upper[0:20]
    one[...] = upper[20:40]
    two[...] = lower[0:20]
    three[...] = lower[20:40]


def final_body(place_ref, *refs):
    on_first = place_ref[3] == 0
    blocks, outs = refs[:8], refs[8:]
    for first, columns in ((0, slice(0, WIDTH_A)), (4, slice(WIDTH_A, WIDTH_A + WIDTH_B))):
        total = blocks[first][...]
        for other in range(1, 4):
            total += blocks[first + other][...]
        low, high = total[0:10], total[10:20]
        outs[0][:, columns] = jnp.where(on_first, low, high)
        outs[1][:, columns] = jnp.where(on_first, high, low)


def assemble_body(place_ref, here, theirs, qkv_ref, out_ref, gain_ref):
    first = place_ref[3] == 0
    left = jnp.where(first, here[...], theirs[...]) * FACTOR
    right = jnp.where(first, theirs[...], here[...]) * FACTOR
    for which, value in enumerate((left, right)):
        out_ref[:, which * HALF:(which + 1) * HALF] = value[:, WIDTH_A:WIDTH_A + HALF]
        for part in range(3):
            at = part * D + which * HALF
            qkv_ref[:, at:at + HALF] = value[:, part * HALF:(part + 1) * HALF]
    both = left[:, WIDTH_A + HALF:] + right[:, WIDTH_A + HALF:]
    column = jnp.sum(both, axis=-1, keepdims=True)
    row = lax.broadcasted_iota(jnp.int32, (10, 10), 0)
    lane = lax.broadcasted_iota(jnp.int32, (10, 10), 1)
    gain_ref[...] = jnp.sum(jnp.where(row == lane, column, 0.0), axis=0, keepdims=True)


def send(value, order, level, step):
    pairs = []
    for source in range(128):
        spots = {
            "z": source // 32, "x": source // 16 % 2 + source // 8 % 2 * 2, "y": source // 2 % 4
        }
        axis = order[source % 2][level]
        spots[axis] = (spots[axis] + step) % 4
        column = spots["x"] % 2 * 2 + spots["x"] // 2
        target = ((spots["z"] * 4 + column) * 4 + spots["y"]) * 2 + source % 2
        pairs.append((source, target))
    return lax.ppermute(value, ("z", "xl", "xh", "y", "c"), pairs)


def swap(value):
    return lax.ppermute(value, "c", [(0, 1), (1, 0)])


def split_body(x_ref, cot_ref, out_ref, sems):
    copies = [
        pltpu.make_async_copy(value.at[frame], out_ref.at[:, which, frame], sems.at[which, frame])
        for which, value in enumerate((x_ref, cot_ref))
        for frame in range(4)
    ]
    for copy in copies:
        copy.start()
    for copy in copies:
        copy.wait()


def join_body(value_ref, after_ref, out_ref, token_ref, sems):
    copies = [
        pltpu.make_async_copy(value_ref.at[:, frame], out_ref.at[frame], sems.at[frame])
        for frame in range(4)
    ]
    for copy in copies:
        copy.start()
    token_ref[...] = after_ref[...]
    for copy in copies:
        copy.wait()


def on_device(activations, grad_out, norm_gain, qkv_weight, out_weight):
    anywhere = pl.BlockSpec(memory_space=pl.ANY)
    in_vmem = pl.BlockSpec(memory_space=pltpu.VMEM)
    params = pltpu.CompilerParams(vmem_limit_bytes=16 * 2**20)
    x_place = lax.axis_index("xh") * 2 + lax.axis_index("xl")
    place = jnp.stack([lax.axis_index("z"), x_place, lax.axis_index("y"), lax.axis_index("c")])
    place = place.astype(jnp.int32)
    group = place[3:]
    gain_row = norm_gain.reshape(1, D)
    both = pl.pallas_call(
        split_body, out_shape=pltpu.VMEM((8, 2, 4, 8, D), BF16), in_specs=[anywhere] * 2,
        out_specs=in_vmem, scratch_shapes=[pltpu.SemaphoreType.DMA((2, 4))],
        compiler_params=params,
    )(from_hbm(activations.reshape(4, 8, 8, D)), from_hbm(grad_out.reshape(4, 8, 8, D)))
    pick_a, pick_b, pick_att, token = pl.pallas_call(
        ready_body, out_shape=[pltpu.HBM((D, D), BF16)] * 3 + [shape(8, 128, F32)],
        in_specs=[pl.BlockSpec(memory_space=pltpu.SMEM)], out_specs=[in_vmem] * 4,
        compiler_params=params,
        cost_estimate=pl.CostEstimate(flops=10**9, bytes_accessed=2 * 10**7, transcendentals=0),
    )(place)
    both = lax.all_to_all(both, ("z", "xl"), split_axis=0, concat_axis=0, tiled=True)
    both = both.reshape(8, 64, D)
    (gained, qkv, cot_other, weight), token = call(
        forward_body,
        [shape(TOKENS, D), shape(TOKENS, 3 * D), shape(TOKENS, HALF), shape(D, 3 * D)],
        [place, both, gain_row, qkv_weight], scalars=1, flops=2 * TOKENS * D * 3 * D,
        scratch=[pltpu.SemaphoreType.DMA((6,))], hbm=(3,), after=[token],
    )
    their_gained, their_cot = swap(gained), swap(cot_other)

    def attention(which, after):
        return call(
            attention_body, [shape(TOKENS, HALF), shape(TOKENS, 3 * HALF)],
            [which, qkv, both, out_weight], scalars=1, flops=5 * 10**9,
            scratch=[pltpu.VMEM((TOKENS, HALF), BF16), pltpu.VMEM((TOKENS, TOKENS), F32)],
            after=after,
        )

    (att_other, stack_other), token = attention(1 - group, token)
    their_stack, their_other = swap(stack_other), swap(att_other)
    (att_mine, stack), token = attention(group, token)
    their_mine = swap(att_mine)
    (gained_a,), token = call(
        gained_body, [shape(D, 512)], [pick_a, gained, their_gained], flops=2 * D * D * 512,
        after=token,
    )
    work = {"a": 10**7, "b": 15 * 10**8, "b second": 8 * 10**9}
    base = {"a": [gained_a, stack, their_stack]}
    kinds = {"a": (term_a, 0, WIDTH_A, ORDER_A), "b": (term_b, 1, HALF, ORDER_B)}

    def run(which, body, outs, extra, after):
        term, scalars, _, _ = kinds[which]
        return call(
            functools.partial(body, term, len(base[which])), outs, base[which] + extra,
            scalars=scalars, flops=work[which], after=after,
        )

    def exchange(which, sent, level):
        order = kinds[which][3]
        return [send(sent[0], order, level, 1), send(sent[1], order, level, 3)]

    state = {}

    def early(which, after):
        sent, after = run(which, early_body, [shape(320, kinds[which][2])] * 2, [], after)
        state[which] = exchange(which, sent, 0)
        return after

    def relay(which, after):
        width, first = kinds[which][2], state[which]
        sent, after = run(which, relay_body, [shape(160, width)] * 2, first, after)
        state[which] = (first, exchange(which, sent, 0))
        return after

    def own_rows(which, after):
        first, second = state[which]
        outs = [shape(320, kinds[which][2], F32)]
        own, after = run(which, own_body, outs, first, after)
        state[which] = own + second
        return after

    gains = {"a": [], "b": []}

    def second_early(which, after):
        width = kinds[which][2] + (128 if gains[which] else 0)
        outs = [shape(rows, width, F32) for rows in (160, 80, 80)]
        (rest, *sent), after = call(
            second_early_body, outs, state[which] + gains[which], after=after,
            flops=work["b second" if which == "b" else "a"],
        )
        state[which] = [rest] + exchange(which, sent, 1)
        return after

    def second_relay(which, after):
        width = state[which][0].shape[1]
        outs = [shape(40, width, F32)] * 2 + [shape(80, width, F32)]
        (plus, minus, part), after = call(
            second_relay_body, outs, state[which], flops=work[which], after=after
        )
        state[which] = [part] + exchange(which, (plus, minus), 1)
        return after

    def third(which, after):
        outs = [shape(20, state[which][0].shape[1], F32)] * 4
        (own, *others), after = call(
            third_body, outs, state[which], flops=10**6, after=after
        )
        order = kinds[which][3]
        sent = [send(other, order, 2, step + 1) for step, other in enumerate(others)]
        state[which] = [own] + sent
        return after

    token = early("a", token)
    (att,), token = call(
        turn_body, [shape(D, 512)], [pick_att, att_mine, att_other, their_mine, their_other],
        after=token,
    )
    base["b"] = [place, both, their_cot, att]
    token = early("b", token)
    (grad_here, keep, give), token = call(
        input_grad_body, [shape(TOKENS, D)] + [shape(8, 384, F32)] * 2,
        [place, both, gain_row, weight, stack, stack_other, pick_b], scalars=1, after=token,
        scratch=[pltpu.VMEM((TOKENS, 3 * D), BF16)],
    )
    arrived = lax.ppermute(give, "xh", [(0, 1), (1, 0)])
    token = own_rows("a", relay("a", token))
    token = relay("b", token + [arrived])
    (own, give), token = call(gain_body, [shape(8, 384, F32)] * 2, [keep, arrived], after=token)
    gains["b"] = [own, lax.ppermute(give, "xl", [(0, 1), (1, 0)])]
    token = own_rows("b", token)
    token = second_early("b", second_early("a", token))
    grad_here, token = late(grad_here, token)
    back = lax.all_to_all(
        grad_here.reshape(8, 4, 8, D), ("z", "xl"), split_axis=0, concat_axis=0, tiled=True
    )
    token = second_relay("b", second_relay("a", token))
    token = third("b", third("a", token))
    grad_tokens, token = pl.pallas_call(
        join_body,
        out_shape=[jax.ShapeDtypeStruct((4, 8, 8, D), BF16), pltpu.VMEM((8, 128), F32)],
        in_specs=[anywhere, in_vmem], out_specs=[anywhere, in_vmem],
        scratch_shapes=[pltpu.SemaphoreType.DMA((4,))], compiler_params=params,
        cost_estimate=pl.CostEstimate(flops=10**7, bytes_accessed=1, transcendentals=0),
    )(back, pltpu.with_memory_space_constraint(token[0], pltpu.VMEM))
    (here, other), token = call(
        final_body, [shape(10, WIDTH_A + WIDTH_B, F32)] * 2, [place] + state["a"] + state["b"],
        scalars=1, after=[token],
    )
    theirs = swap(other)
    (qkv_grad, out_grad, gain_grad), _ = call(
        assemble_body, [shape(10, 3 * D, F32), shape(10, D, F32), shape(1, 10, F32)],
        [place, here, theirs], scalars=1, results=jax.ShapeDtypeStruct, last=True,
        after=token,
    )
    return (grad_tokens.reshape(1, 4, 64, D), qkv_grad, out_grad, gain_grad.reshape(10))


def solution(mesh):
    fine = Mesh(mesh.devices.reshape(4, 2, 2, 4, 2), ("z", "xl", "xh", "y", "c"))
    tm, space = ("z", "xl"), ("xh", "y", "c")
    tokens = P(None, tm, space, None)
    in_specs = (tokens, tokens, P(), P(), P())
    out_specs = (tokens, P(tm + space, None), P(tm + space, None), P(tm + space))
    return jax.shard_map(
        on_device, mesh=fine, in_specs=in_specs, out_specs=out_specs, check_vma=False
    )
```

```python
import functools
import math

import jax
import jax.numpy as jnp
from jax import lax
from jax.experimental import pallas as pl
from jax.experimental.pallas import tpu as pltpu
from jax.sharding import Mesh, PartitionSpec as P

D = 1280
HEADS = 16
HEAD = 80
HALF = 640
TOKENS = 256
INVERSE_ROOT = 1.0 / math.sqrt(HEAD)
FACTOR = 1.0 / math.sqrt(32 * 1024)
BF16, F32 = jnp.bfloat16, jnp.float32
ORDER_A = (("z", "y", "x"), ("y", "x", "z"))
ORDER_B = (("x", "y", "z"), ("x", "y", "z"))
WIDTH_A, WIDTH_B = 1920, 768
NN = (((1,), (0,)), ((), ()))
NT = (((1,), (1,)), ((), ()))
TN = (((0,), (0,)), ((), ()))


def dot(left, right, dims=NN):
    return lax.dot_general(left, right, dims, preferred_element_type=F32)


def call(body, outs, operands, scalars=0, flops=0, scratch=(), after=None, results=pltpu.VMEM,
         hbm=(), last=False):
    vmem = pl.BlockSpec(memory_space=pltpu.VMEM)
    smem = pl.BlockSpec(memory_space=pltpu.SMEM)
    count, tokens = len(operands), [] if last else [pltpu.VMEM((8, 128), F32)]
    size = sum(math.prod(o.shape) * o.dtype.itemsize for o in list(operands) + list(outs))
    given = list(operands) + ([] if after is None else list(after))
    spaces = [smem] * scalars + [vmem] * (len(given) - scalars)
    placed = [
        value if place < scalars else pltpu.with_memory_space_constraint(value, pltpu.VMEM)
        for place, value in enumerate(given)
    ]
    for place in hbm:
        spaces[place] = pl.BlockSpec(memory_space=pl.ANY)
        placed[place] = from_hbm(given[place])

    def run(*refs):
        results, rest = refs[len(placed):len(placed) + len(outs)], refs[len(placed) + len(outs):]
        if not last:
            rest[0][...] = jnp.zeros((8, 128), F32)
            rest = rest[1:]
        body(*refs[:count], *results, *rest)

    given = pl.pallas_call(
        run,
        out_shape=[results(o.shape, o.dtype) for o in outs] + tokens,
        in_specs=spaces,
        out_specs=[vmem] * (len(outs) + len(tokens)),
        scratch_shapes=scratch,
        compiler_params=pltpu.CompilerParams(vmem_limit_bytes=16 * 2**20),
        cost_estimate=pl.CostEstimate(
            flops=flops, bytes_accessed=size // 4 if flops else 1, transcendentals=0
        ),
    )(*placed)
    return list(given[:len(outs)]), list(given[len(outs):])


def late(value, after):
    vmem, anywhere = pl.BlockSpec(memory_space=pltpu.VMEM), pl.BlockSpec(memory_space=pl.ANY)

    def body(*refs):
        refs[-1][...] = jnp.zeros((8, 128), F32)

    value, token = pl.pallas_call(
        body,
        out_shape=[jax.ShapeDtypeStruct(value.shape, value.dtype), pltpu.VMEM((8, 128), F32)],
        in_specs=[anywhere] + [vmem] * len(after), out_specs=[anywhere, vmem],
        input_output_aliases={0: 0},
        compiler_params=pltpu.CompilerParams(vmem_limit_bytes=2**20),
        cost_estimate=pl.CostEstimate(flops=10**7, bytes_accessed=1, transcendentals=0),
    )(value, *[pltpu.with_memory_space_constraint(array, pltpu.VMEM) for array in after])
    return value, [token]


def from_hbm(value):
    return pltpu.with_memory_space_constraint(value, pltpu.HBM)


def shape(rows, columns, kind=BF16):
    return jax.ShapeDtypeStruct((rows, columns), kind)


def side(both_ref, which, columns=slice(None)):
    value = both_ref[:, 32 * which:32 * which + 32, columns]
    return value.reshape(TOKENS, value.shape[-1])


def normalize(both_ref):
    x_wide = side(both_ref, 0).astype(F32)
    centred = x_wide - jnp.mean(x_wide, axis=-1, keepdims=True)
    variance = jnp.mean(centred * centred, axis=-1, keepdims=True)
    inv_std = lax.rsqrt(variance + 1e-06)
    return centred * inv_std, inv_std


def half(place_ref, own):
    core = place_ref[3] if own else 1 - place_ref[3]
    return pl.ds(pl.multiple_of(core * HALF, 128), HALF)


def forward_body(place_ref, both_ref, gain_ref, weight_ref, gained_ref, qkv_ref, cot_ref,
                 held_ref, hat_ref, inv_ref, sems):
    pieces = [slice(step * HALF, (step + 1) * HALF) for step in range(6)]
    copies = [
        pltpu.make_async_copy(weight_ref.at[:, piece], held_ref.at[:, piece], sems.at[step])
        for step, piece in enumerate(pieces)
    ]
    for copy in copies[:2]:
        copy.start()
    normalized, inv_std = normalize(both_ref)
    hat_ref[...] = normalized
    inv_ref[...] = jnp.broadcast_to(inv_std, (TOKENS, 128))
    gained = (normalized * gain_ref[...]).astype(BF16)
    gained_ref[...] = gained
    cot_ref[...] = side(both_ref, 1, half(place_ref, False))
    for step, (copy, piece) in enumerate(zip(copies, pieces)):
        copy.wait()
        if step + 2 < len(copies):
            copies[step + 2].start()
        qkv_ref[:, piece] = dot(gained, held_ref[:, piece]).astype(BF16)


def attention_body(group_ref, qkv_ref, both_ref, weight_ref, att_ref, stack_ref, ag_ref,
                   bias_ref):
    start = pl.multiple_of(group_ref[0] * HALF, 128)
    ag_ref[...] = dot(side(both_ref, 1), weight_ref[pl.ds(start, HALF), :], NT).astype(BF16)
    row = lax.broadcasted_iota(jnp.int32, (TOKENS, TOKENS), 0)
    column = lax.broadcasted_iota(jnp.int32, (TOKENS, TOKENS), 1)
    bias_ref[...] = jnp.where((row & 7) == (column & 7), 0.0, -1e30)
    tiles = [[[] for _ in range(5)] for _ in range(4)]
    for head in range(8):
        low, high = head * HEAD, (head + 1) * HEAD
        first, last = low // 128 * 128, -(-high // 128) * 128
        width = last - first
        lanes = lax.broadcasted_iota(jnp.int32, (1, width), 1) + first
        keep = jnp.where((lanes >= low) & (lanes < high), 1.0, 0.0).astype(BF16)

        def cut(part):
            return qkv_ref[:, pl.ds(pl.multiple_of(start + part * D + first, 128), width)] * keep

        query, key, value = cut(0), cut(1), cut(2)
        grad = ag_ref[:, first:last] * keep
        scores = dot(key, query, NT) + bias_ref[...]
        shifted = jnp.exp((scores - jnp.max(scores, axis=0, keepdims=True)) * INVERSE_ROOT)
        prob = shifted * (1.0 / jnp.sum(shifted, axis=0, keepdims=True))
        prob_low = prob.astype(BF16)
        prob_grad = dot(value, grad, NT)
        mixed = jnp.sum(prob_grad * prob, axis=0, keepdims=True)
        score_grad = (prob * (prob_grad - mixed) * INVERSE_ROOT).astype(BF16)
        results = (
            dot(prob_low, value, TN), dot(score_grad, key, TN), dot(score_grad, query),
            dot(prob_low, grad),
        )
        for kind, result in enumerate(results):
            for tile in range(width // 128):
                piece = result[:, tile * 128:(tile + 1) * 128]
                tiles[kind][first // 128 + tile].append(piece)
    for kind in range(4):
        for tile in range(5):
            total = sum(tiles[kind][tile][1:], tiles[kind][tile][0]).astype(BF16)
            if kind == 0:
                att_ref[:, tile * 128:(tile + 1) * 128] = total
            else:
                at = (kind - 1) * HALF + tile * 128
                stack_ref[:, at:at + 128] = total


def joint_attention_body(group_ref, qkv_ref, both_ref, weight_ref, out_ref, *scratch):
    attention_body(
        group_ref, qkv_ref, both_ref, weight_ref, out_ref.at[:, :HALF], out_ref.at[:, HALF:],
        *scratch
    )


def input_grad_body(place_ref, both_ref, hat_ref, inv_ref, gain_ref, weight_ref, mine_ref,
                    other_ref, pick_ref,
                    grad_ref, keep, give, joined_ref):
    for own, stack_ref in ((True, mine_ref), (False, other_ref)):
        group = place_ref[3] if own else 1 - place_ref[3]
        for part in range(3):
            columns = pl.ds(pl.multiple_of(group * HALF + part * D, 128), HALF)
            start = part * HALF if own else (part + 1) * HALF
            joined_ref[:, columns] = stack_ref[:, start:start + HALF]
    normed_grad = dot(joined_ref[...], weight_ref[...], NT)
    normalized, inv_std = hat_ref[...], inv_ref[:, 0:1]
    scaled = normed_grad * gain_ref[...]
    inner = scaled - jnp.mean(scaled, axis=-1, keepdims=True)
    inner -= normalized * jnp.mean(scaled * normalized, axis=-1, keepdims=True)
    grad_ref[...] = (side(both_ref, 1).astype(F32) + inv_std * inner).astype(BF16)
    gain = jnp.sum(normed_grad * normalized, axis=0, keepdims=True)
    high = gain.astype(BF16).astype(F32)
    middle = (gain - high).astype(BF16).astype(F32)
    row = lax.broadcasted_iota(jnp.int32, (16, D), 0)
    split = jnp.where(row == 2, gain - high - middle, 0.0)
    split = jnp.where(row == 0, high, jnp.where(row == 1, middle, split)).astype(BF16)
    blocks = []
    for block in range(4):
        rows = slice(block * 320, (block + 1) * 320)
        ordered = jnp.sum(dot(split, pick_ref[rows, :], NT), axis=0, keepdims=True)
        blocks.append(jnp.concatenate([ordered, jnp.zeros((1, 64), F32)], axis=1))
    even = (place_ref[1] & 1) == 0
    near = jnp.where(even, blocks[1], blocks[3])
    far = jnp.where(even, blocks[3], blocks[1])
    rest = jnp.zeros((6, 384), F32)
    keep[...] = jnp.concatenate([blocks[0], near, rest], axis=0)
    give[...] = jnp.concatenate([blocks[2], far, rest], axis=0)


def gain_body(keep, arrived, own, give):
    total = keep[...] + arrived[...]
    own[...] = total
    give[...] = jnp.concatenate([total[1:8], total[0:1]], axis=0)


def pick(source):
    lanes = lax.broadcasted_iota(jnp.int32, (source.shape[0], D), 1)
    return jnp.where(lanes == source, 1.0, 0.0).astype(BF16)


def relative_rows(place_ref, order, block):
    here = {"z": place_ref[0], "x": place_ref[1], "y": place_ref[2]}
    on_first = place_ref[3] == 0
    row = lax.broadcasted_iota(jnp.int32, (320, 1), 0)

    def count(value, size):
        return sum(jnp.where(value >= size * step, 1, 0) for step in (1, 2, 3))

    def offset(axis, at):
        if axis == "x":
            return (at & 1) * 160 + (at >> 1) * 80
        return at * (320 if axis == "z" else 20)

    second = count(row, 80)
    row = row - 80 * second
    third = count(row, 20)
    row = row - 20 * third
    for level, step in enumerate((block, second, third)):
        one, two = (
            offset(axes[level], (here[axes[level]] + step) & 3) for axes in order
        )
        row = row + jnp.where(on_first, one, two)
    return row


def ready_body(place_ref, pick_a, pick_b, pick_att, token):
    token[...] = jnp.zeros((8, 128), F32)
    for step in range(4):
        rows = slice(step * 320, (step + 1) * 320)
        pick_a[rows, :] = pick(relative_rows(place_ref, ORDER_A, step))
        feature = relative_rows(place_ref, ORDER_B, step)
        pick_b[rows, :] = pick(feature)
        feature = feature + place_ref[3] * HALF
        pick_att[rows, :] = pick(jnp.where(feature >= D, feature - D, feature))


def gained_body(pick_ref, own_ref, partner_ref, out):
    for step in range(4):
        rows = slice(step * 320, (step + 1) * 320)
        out[rows, :TOKENS] = dot(pick_ref[rows, :], own_ref[...], NT).astype(BF16)
        out[rows, TOKENS:] = dot(pick_ref[rows, :], partner_ref[...], NT).astype(BF16)


def turn_body(pick_att, mine, other, their_mine, theirs, att_out):
    sides = ((mine, other), (theirs, their_mine))
    for step in range(4):
        rows = slice(step * 320, (step + 1) * 320)
        for which, (first, second) in enumerate(sides):
            turned = dot(pick_att[rows, :HALF], first[:, :HALF], NT)
            turned += dot(pick_att[rows, HALF:], second[:, :HALF], NT)
            att_out[rows, which * TOKENS:(which + 1) * TOKENS] = turned.astype(BF16)


def term_a(rows, gained, stack, theirs):
    return dot(gained[rows, :TOKENS], stack[...]) + dot(gained[rows, TOKENS:], theirs[:, HALF:])


def term_b(rows, place_ref, both, their_cot, att):
    outer = dot(att[rows, :TOKENS], side(both, 1, half(place_ref, True)))
    return outer + dot(att[rows, TOKENS:], their_cot[...])


def early_body(term, count, *refs):
    plus, minus = refs[count:]
    far = term(slice(640, 960), *refs[:count])
    plus[0:160, :] = far[0:160].astype(BF16)
    minus[0:160, :] = far[160:320].astype(BF16)
    plus[160:320, :] = term(slice(480, 640), *refs[:count]).astype(BF16)
    minus[160:320, :] = term(slice(960, 1120), *refs[:count]).astype(BF16)


def relay_body(term, count, *refs):
    from_minus, from_plus, plus, minus = refs[count:]
    up = term(slice(320, 480), *refs[:count]) + from_minus[0:160, :].astype(F32)
    down = term(slice(1120, 1280), *refs[:count]) + from_plus[0:160, :].astype(F32)
    plus[...] = up.astype(BF16)
    minus[...] = down.astype(BF16)


def own_body(term, count, *refs):
    from_minus, from_plus, own = refs[count:]
    total = term(slice(0, 320), *refs[:count])
    own[0:160, :] = total[0:160] + from_plus[160:320, :].astype(F32)
    own[160:320, :] = total[160:320] + from_minus[160:320, :].astype(F32)


def second_early_body(own, from_minus, from_plus, *refs):
    gains, (rest, plus, minus) = refs[:-3], refs[-3:]
    upper = own[0:160, :] + from_minus[...].astype(F32)
    lower = own[160:320, :] + from_plus[...].astype(F32)
    if gains:
        line = gains[0][0:1, :] + gains[1][0:1, :]
        row = lax.broadcasted_iota(jnp.int32, (320, 384), 0)
        lane = lax.broadcasted_iota(jnp.int32, (320, 384), 1)
        column = jnp.sum(jnp.where(row == lane, line, 0.0), axis=-1, keepdims=True)
        column = jnp.where(lane[:, :128] == 0, column, 0.0)
        upper = jnp.concatenate([upper, column[0:160]], axis=1)
        lower = jnp.concatenate([lower, column[160:320]], axis=1)
    rest[0:120, :] = upper[0:120]
    plus[40:80, :] = upper[120:160]
    plus[0:40, :] = lower[0:40]
    minus[0:80, :] = lower[40:120]
    rest[120:160, :] = lower[120:160]


def second_relay_body(rest, from_minus, from_plus, plus, minus, part):
    plus[...] = rest[80:120, :] + from_minus[0:40, :]
    minus[...] = rest[120:160, :] + from_plus[0:40, :]
    part[0:40, :] = rest[0:40, :] + from_plus[40:80, :]
    part[40:80, :] = rest[40:80, :] + from_minus[40:80, :]


def third_body(part, last_minus, last_plus, own, one, two, three):
    upper = part[0:40, :] + last_minus[...]
    lower = part[40:80, :] + last_plus[...]
    own[...] = upper[0:20]
    one[...] = upper[20:40]
    two[...] = lower[0:20]
    three[...] = lower[20:40]


def add_body(own, one, two, three, out):
    out[...] = (own[...] + one[...]) + (two[...] + three[...])


def final_body(place_ref, total_a, own, one, two, three, here, other):
    on_first = place_ref[3] == 0
    total_b = (own[...] + one[...]) + (two[...] + three[...])
    total = jnp.concatenate([total_a[...], total_b], axis=1)
    low, high = total[0:10], total[10:20]
    here[...] = jnp.where(on_first, low, high)
    other[...] = jnp.where(on_first, high, low)


def assemble_body(place_ref, here, theirs, qkv_ref, out_ref, gain_ref):
    first = place_ref[3] == 0
    left = jnp.where(first, here[...], theirs[...]) * FACTOR
    right = jnp.where(first, theirs[...], here[...]) * FACTOR
    for which, value in enumerate((left, right)):
        out_ref[:, which * HALF:(which + 1) * HALF] = value[:, WIDTH_A:WIDTH_A + HALF]
        for part in range(3):
            at = part * D + which * HALF
            qkv_ref[:, at:at + HALF] = value[:, part * HALF:(part + 1) * HALF]
    both = left[:, WIDTH_A + HALF:] + right[:, WIDTH_A + HALF:]
    column = jnp.sum(both, axis=-1, keepdims=True)
    row = lax.broadcasted_iota(jnp.int32, (10, 10), 0)
    lane = lax.broadcasted_iota(jnp.int32, (10, 10), 1)
    gain_ref[...] = jnp.sum(jnp.where(row == lane, column, 0.0), axis=0, keepdims=True)


def send(value, order, level, step):
    pairs = []
    for source in range(128):
        spots = {
            "z": source // 32, "x": source // 16 % 2 + source // 8 % 2 * 2, "y": source // 2 % 4
        }
        axis = order[source % 2][level]
        spots[axis] = (spots[axis] + step) % 4
        column = spots["x"] % 2 * 2 + spots["x"] // 2
        target = ((spots["z"] * 4 + column) * 4 + spots["y"]) * 2 + source % 2
        pairs.append((source, target))
    return lax.ppermute(value, ("z", "xl", "xh", "y", "c"), pairs)


def swap(value):
    return lax.ppermute(value, "c", [(0, 1), (1, 0)])


def split_body(x_ref, cot_ref, out_ref, sems):
    copies = [
        pltpu.make_async_copy(value.at[frame], out_ref.at[:, which, frame], sems.at[which, frame])
        for which, value in enumerate((x_ref, cot_ref))
        for frame in range(4)
    ]
    for copy in copies:
        copy.start()
    for copy in copies:
        copy.wait()


def join_body(value_ref, after_ref, out_ref, token_ref, sems):
    copies = [
        pltpu.make_async_copy(value_ref.at[:, frame], out_ref.at[frame], sems.at[frame])
        for frame in range(4)
    ]
    for copy in copies:
        copy.start()
    token_ref[...] = after_ref[...]
    for copy in copies:
        copy.wait()


def on_device(activations, grad_out, norm_gain, qkv_weight, out_weight):
    anywhere = pl.BlockSpec(memory_space=pl.ANY)
    in_vmem = pl.BlockSpec(memory_space=pltpu.VMEM)
    params = pltpu.CompilerParams(vmem_limit_bytes=16 * 2**20)
    x_place = lax.axis_index("xh") * 2 + lax.axis_index("xl")
    place = jnp.stack([lax.axis_index("z"), x_place, lax.axis_index("y"), lax.axis_index("c")])
    place = place.astype(jnp.int32)
    group = place[3:]
    gain_row = norm_gain.reshape(1, D)
    both = pl.pallas_call(
        split_body, out_shape=pltpu.VMEM((8, 2, 4, 8, D), BF16), in_specs=[anywhere] * 2,
        out_specs=in_vmem, scratch_shapes=[pltpu.SemaphoreType.DMA((2, 4))],
        compiler_params=params,
    )(from_hbm(activations.reshape(4, 8, 8, D)), from_hbm(grad_out.reshape(4, 8, 8, D)))
    pick_a, pick_b, pick_att, token = pl.pallas_call(
        ready_body, out_shape=[pltpu.HBM((D, D), BF16)] * 3 + [shape(8, 128, F32)],
        in_specs=[pl.BlockSpec(memory_space=pltpu.SMEM)], out_specs=[in_vmem] * 4,
        compiler_params=params,
        cost_estimate=pl.CostEstimate(flops=10**9, bytes_accessed=2 * 10**7, transcendentals=0),
    )(place)
    both = lax.all_to_all(both, ("z", "xl"), split_axis=0, concat_axis=0, tiled=True)
    both = both.reshape(8, 64, D)
    (gained, qkv, cot_other, weight, hat, inv_std), token = call(
        forward_body,
        [shape(TOKENS, D), shape(TOKENS, 3 * D), shape(TOKENS, HALF), shape(D, 3 * D),
         shape(TOKENS, D, F32), shape(TOKENS, 128, F32)],
        [place, both, gain_row, qkv_weight], scalars=1, flops=2 * TOKENS * D * 3 * D,
        scratch=[pltpu.SemaphoreType.DMA((6,))], hbm=(3,), after=[token],
    )
    their_gained, their_cot = swap(gained), swap(cot_other)

    def attention(which, after, outs):
        return call(
            attention_body if len(outs) == 2 else joint_attention_body, outs,
            [which, qkv, both, out_weight], scalars=1, flops=5 * 10**9,
            scratch=[pltpu.VMEM((TOKENS, HALF), BF16), pltpu.VMEM((TOKENS, TOKENS), F32)],
            after=after,
        )

    (other_half,), token = attention(1 - group, token, [shape(TOKENS, 4 * HALF)])
    their_half = swap(other_half)
    (att_mine, stack), token = attention(
        group, token, [shape(TOKENS, HALF), shape(TOKENS, 3 * HALF)]
    )
    their_mine = swap(att_mine)
    (gained_a,), token = call(
        gained_body, [shape(D, 512)], [pick_a, gained, their_gained], flops=2 * D * D * 512,
        after=token,
    )
    work = {"a": 10**7, "b": 15 * 10**8, "b second": 8 * 10**9}
    base = {"a": [gained_a, stack, their_half]}
    kinds = {"a": (term_a, 0, WIDTH_A, ORDER_A), "b": (term_b, 1, HALF, ORDER_B)}

    def run(which, body, outs, extra, after):
        term, scalars, _, _ = kinds[which]
        return call(
            functools.partial(body, term, len(base[which])), outs, base[which] + extra,
            scalars=scalars, flops=work[which], after=after,
        )

    def exchange(which, sent, level):
        order = kinds[which][3]
        return [send(sent[0], order, level, 1), send(sent[1], order, level, 3)]

    state = {}

    def early(which, after):
        sent, after = run(which, early_body, [shape(320, kinds[which][2])] * 2, [], after)
        state[which] = exchange(which, sent, 0)
        return after

    def relay(which, after):
        width, first = kinds[which][2], state[which]
        sent, after = run(which, relay_body, [shape(160, width)] * 2, first, after)
        state[which] = (first, exchange(which, sent, 0))
        return after

    def own_rows(which, after):
        first, second = state[which]
        outs = [shape(320, kinds[which][2], F32)]
        own, after = run(which, own_body, outs, first, after)
        state[which] = own + second
        return after

    gains = {"a": [], "b": []}

    def second_early(which, after):
        width = kinds[which][2] + (128 if gains[which] else 0)
        outs = [shape(rows, width, F32) for rows in (160, 80, 80)]
        (rest, *sent), after = call(
            second_early_body, outs, state[which] + gains[which], after=after,
            flops=work["b second" if which == "b" else "a"],
        )
        state[which] = [rest] + exchange(which, sent, 1)
        return after

    def second_relay(which, after):
        width = state[which][0].shape[1]
        outs = [shape(40, width, F32)] * 2 + [shape(80, width, F32)]
        (plus, minus, part), after = call(
            second_relay_body, outs, state[which], flops=work[which], after=after
        )
        state[which] = [part] + exchange(which, (plus, minus), 1)
        return after

    def third(which, after):
        outs = [shape(20, state[which][0].shape[1], F32)] * 4
        (own, *others), after = call(
            third_body, outs, state[which], flops=work[which], after=after
        )
        order = kinds[which][3]
        sent = [send(other, order, 2, step + 1) for step, other in enumerate(others)]
        state[which] = [own] + sent
        return after

    token = early("a", token + [their_mine])
    (att,), token = call(
        turn_body, [shape(D, 512)], [pick_att, att_mine, other_half, their_mine, their_half],
        after=token,
    )
    base["b"] = [place, both, their_cot, att]
    token = early("b", token)
    (grad_here, keep, give), token = call(
        input_grad_body, [shape(TOKENS, D)] + [shape(8, 384, F32)] * 2,
        [place, both, hat, inv_std, gain_row, weight, stack, other_half, pick_b], scalars=1,
        after=token,
        scratch=[pltpu.VMEM((TOKENS, 3 * D), BF16)],
    )
    arrived = lax.ppermute(give, "xh", [(0, 1), (1, 0)])
    token = relay("b", relay("a", token))
    token = own_rows("b", own_rows("a", token))
    (own, give), token = call(gain_body, [shape(8, 384, F32)] * 2, [keep, arrived], after=token)
    gains["b"] = [own, lax.ppermute(give, "xl", [(0, 1), (1, 0)])]
    token = second_early("b", second_early("a", token))
    grad_here, token = late(grad_here, token)
    back = lax.all_to_all(
        grad_here.reshape(8, 4, 8, D), ("z", "xl"), split_axis=0, concat_axis=0, tiled=True
    )
    token = second_relay("b", second_relay("a", token))
    token = third("b", third("a", token))
    (total_a,), token = call(add_body, [shape(20, WIDTH_A, F32)], state["a"], after=token)
    grad_tokens, token = pl.pallas_call(
        join_body,
        out_shape=[jax.ShapeDtypeStruct((4, 8, 8, D), BF16), pltpu.VMEM((8, 128), F32)],
        in_specs=[anywhere, in_vmem], out_specs=[anywhere, in_vmem],
        scratch_shapes=[pltpu.SemaphoreType.DMA((4,))], compiler_params=params,
        cost_estimate=pl.CostEstimate(flops=10**7, bytes_accessed=1, transcendentals=0),
    )(back, pltpu.with_memory_space_constraint(token[0], pltpu.VMEM))
    (here, other), token = call(
        final_body, [shape(10, WIDTH_A + WIDTH_B, F32)] * 2, [place, total_a] + state["b"],
        scalars=1, after=[token],
    )
    theirs = swap(other)
    (qkv_grad, out_grad, gain_grad), _ = call(
        assemble_body, [shape(10, 3 * D, F32), shape(10, D, F32), shape(1, 10, F32)],
        [place, here, theirs], scalars=1, results=jax.ShapeDtypeStruct, last=True,
        after=token,
    )
    return (grad_tokens.reshape(1, 4, 64, D), qkv_grad, out_grad, gain_grad.reshape(10))


def solution(mesh):
    fine = Mesh(mesh.devices.reshape(4, 2, 2, 4, 2), ("z", "xl", "xh", "y", "c"))
    tm, space = ("z", "xl"), ("xh", "y", "c")
    tokens = P(None, tm, space, None)
    in_specs = (tokens, tokens, P(), P(), P())
    out_specs = (tokens, P(tm + space, None), P(tm + space, None), P(tm + space))
    return jax.shard_map(
        on_device, mesh=fine, in_specs=in_specs, out_specs=out_specs, check_vma=False
    )
```

```python
import functools
import math

import jax
import jax.numpy as jnp
from jax import lax
from jax.experimental import pallas as pl
from jax.experimental.pallas import tpu as pltpu
from jax.sharding import Mesh, PartitionSpec as P

D = 1280
HEADS = 16
HEAD = 80
HALF = 640
TOKENS = 256
INVERSE_ROOT = 1.0 / math.sqrt(HEAD)
FACTOR = 1.0 / math.sqrt(32 * 1024)
BF16, F32 = jnp.bfloat16, jnp.float32
ORDER_A = (("z", "y", "x"), ("y", "x", "z"))
ORDER_B = (("x", "y", "z"), ("x", "y", "z"))
WIDTH_A, WIDTH_B = 1920, 768
NN = (((1,), (0,)), ((), ()))
NT = (((1,), (1,)), ((), ()))
TN = (((0,), (0,)), ((), ()))


def dot(left, right, dims=NN):
    return lax.dot_general(left, right, dims, preferred_element_type=F32)


def call(body, outs, operands, scalars=0, flops=0, scratch=(), after=None, results=pltpu.VMEM,
         hbm=(), last=False):
    vmem = pl.BlockSpec(memory_space=pltpu.VMEM)
    smem = pl.BlockSpec(memory_space=pltpu.SMEM)
    count, tokens = len(operands), [] if last else [pltpu.VMEM((8, 128), F32)]
    size = sum(math.prod(o.shape) * o.dtype.itemsize for o in list(operands) + list(outs))
    given = list(operands) + ([] if after is None else list(after))
    spaces = [smem] * scalars + [vmem] * (len(given) - scalars)
    placed = [
        value if place < scalars else pltpu.with_memory_space_constraint(value, pltpu.VMEM)
        for place, value in enumerate(given)
    ]
    for place in hbm:
        spaces[place] = pl.BlockSpec(memory_space=pl.ANY)
        placed[place] = from_hbm(given[place])

    def run(*refs):
        results, rest = refs[len(placed):len(placed) + len(outs)], refs[len(placed) + len(outs):]
        if not last:
            rest[0][...] = jnp.zeros((8, 128), F32)
            rest = rest[1:]
        body(*refs[:count], *results, *rest)

    given = pl.pallas_call(
        run,
        out_shape=[results(o.shape, o.dtype) for o in outs] + tokens,
        in_specs=spaces,
        out_specs=[vmem] * (len(outs) + len(tokens)),
        scratch_shapes=scratch,
        compiler_params=pltpu.CompilerParams(vmem_limit_bytes=16 * 2**20),
        cost_estimate=pl.CostEstimate(
            flops=flops, bytes_accessed=size // 4 if flops else 1, transcendentals=0
        ),
    )(*placed)
    return list(given[:len(outs)]), list(given[len(outs):])


def late(value, after):
    vmem, anywhere = pl.BlockSpec(memory_space=pltpu.VMEM), pl.BlockSpec(memory_space=pl.ANY)

    def body(*refs):
        refs[-1][...] = jnp.zeros((8, 128), F32)

    value, token = pl.pallas_call(
        body,
        out_shape=[jax.ShapeDtypeStruct(value.shape, value.dtype), pltpu.VMEM((8, 128), F32)],
        in_specs=[anywhere] + [vmem] * len(after), out_specs=[anywhere, vmem],
        input_output_aliases={0: 0},
        compiler_params=pltpu.CompilerParams(vmem_limit_bytes=2**20),
        cost_estimate=pl.CostEstimate(flops=10**7, bytes_accessed=1, transcendentals=0),
    )(value, *[pltpu.with_memory_space_constraint(array, pltpu.VMEM) for array in after])
    return value, [token]


def from_hbm(value):
    return pltpu.with_memory_space_constraint(value, pltpu.HBM)


def shape(rows, columns, kind=BF16):
    return jax.ShapeDtypeStruct((rows, columns), kind)


def side(both_ref, which, columns=slice(None)):
    value = both_ref[:, 32 * which:32 * which + 32, columns]
    return value.reshape(TOKENS, value.shape[-1])


def normalize(both_ref):
    x_wide = side(both_ref, 0).astype(F32)
    centred = x_wide - jnp.mean(x_wide, axis=-1, keepdims=True)
    variance = jnp.mean(centred * centred, axis=-1, keepdims=True)
    inv_std = lax.rsqrt(variance + 1e-06)
    return centred * inv_std, inv_std


def half(place_ref, own):
    core = place_ref[3] if own else 1 - place_ref[3]
    return pl.ds(pl.multiple_of(core * HALF, 128), HALF)


def forward_body(place_ref, both_ref, gain_ref, weight_ref, out_weight_ref, gained_ref, qkv_ref, cot_ref,
                 held_ref, hat_ref, inv_ref, out_held_ref, sems):
    pieces = [slice(step * HALF, (step + 1) * HALF) for step in range(6)]
    copies = [
        pltpu.make_async_copy(weight_ref.at[:, piece], held_ref.at[:, piece], sems.at[step])
        for step, piece in enumerate(pieces)
    ]
    copies.append(pltpu.make_async_copy(out_weight_ref, out_held_ref, sems.at[6]))
    for copy in copies[:3]:
        copy.start()
    normalized, inv_std = normalize(both_ref)
    hat_ref[...] = normalized
    inv_ref[...] = jnp.broadcast_to(inv_std, (TOKENS, 128))
    gained = (normalized * gain_ref[...]).astype(BF16)
    gained_ref[...] = gained
    cot_ref[...] = side(both_ref, 1, half(place_ref, False))
    for step, (copy, piece) in enumerate(zip(copies, pieces)):
        copy.wait()
        if step + 3 < len(copies):
            copies[step + 3].start()
        qkv_ref[:, piece] = dot(gained, held_ref[:, piece]).astype(BF16)
    copies[6].wait()


def attention_body(group_ref, qkv_ref, both_ref, weight_ref, att_ref, stack_ref, ag_ref,
                   bias_ref):
    start = pl.multiple_of(group_ref[0] * HALF, 128)
    ag_ref[...] = dot(side(both_ref, 1), weight_ref[pl.ds(start, HALF), :], NT).astype(BF16)
    row = lax.broadcasted_iota(jnp.int32, (TOKENS, TOKENS), 0)
    column = lax.broadcasted_iota(jnp.int32, (TOKENS, TOKENS), 1)
    bias_ref[...] = jnp.where((row & 7) == (column & 7), 0.0, -1e30)
    tiles = [[[] for _ in range(5)] for _ in range(4)]
    for head in range(8):
        low, high = head * HEAD, (head + 1) * HEAD
        first, last = low // 128 * 128, -(-high // 128) * 128
        width = last - first
        lanes = lax.broadcasted_iota(jnp.int32, (1, width), 1) + first
        keep = jnp.where((lanes >= low) & (lanes < high), 1.0, 0.0).astype(BF16)

        def cut(part):
            return qkv_ref[:, pl.ds(pl.multiple_of(start + part * D + first, 128), width)] * keep

        query, key, value = cut(0), cut(1), cut(2)
        grad = ag_ref[:, first:last] * keep
        scores = dot(key, query, NT) + bias_ref[...]
        shifted = jnp.exp((scores - jnp.max(scores, axis=0, keepdims=True)) * INVERSE_ROOT)
        prob = shifted * (1.0 / jnp.sum(shifted, axis=0, keepdims=True))
        prob_low = prob.astype(BF16)
        prob_grad = dot(value, grad, NT)
        mixed = jnp.sum(prob_grad * prob, axis=0, keepdims=True)
        score_grad = (prob * (prob_grad - mixed) * INVERSE_ROOT).astype(BF16)
        results = (
            dot(prob_low, value, TN), dot(score_grad, key, TN), dot(score_grad, query),
            dot(prob_low, grad),
        )
        for kind, result in enumerate(results):
            for tile in range(width // 128):
                piece = result[:, tile * 128:(tile + 1) * 128]
                tiles[kind][first // 128 + tile].append(piece)
    for kind in range(4):
        for tile in range(5):
            total = sum(tiles[kind][tile][1:], tiles[kind][tile][0]).astype(BF16)
            if kind == 0:
                att_ref[:, tile * 128:(tile + 1) * 128] = total
            else:
                at = (kind - 1) * HALF + tile * 128
                stack_ref[:, at:at + 128] = total


def joint_attention_body(group_ref, qkv_ref, both_ref, weight_ref, out_ref, *scratch):
    attention_body(
        group_ref, qkv_ref, both_ref, weight_ref, out_ref.at[:, :HALF], out_ref.at[:, HALF:],
        *scratch
    )


def input_grad_body(place_ref, both_ref, hat_ref, inv_ref, gain_ref, weight_ref, mine_ref,
                    other_ref, pick_ref,
                    grad_ref, keep, give, joined_ref):
    for own, stack_ref in ((True, mine_ref), (False, other_ref)):
        group = place_ref[3] if own else 1 - place_ref[3]
        for part in range(3):
            columns = pl.ds(pl.multiple_of(group * HALF + part * D, 128), HALF)
            start = part * HALF if own else (part + 1) * HALF
            joined_ref[:, columns] = stack_ref[:, start:start + HALF]
    normed_grad = dot(joined_ref[...], weight_ref[...], NT)
    normalized, inv_std = hat_ref[...], inv_ref[:, 0:1]
    scaled = normed_grad * gain_ref[...]
    inner = scaled - jnp.mean(scaled, axis=-1, keepdims=True)
    inner -= normalized * jnp.mean(scaled * normalized, axis=-1, keepdims=True)
    grad_ref[...] = (side(both_ref, 1).astype(F32) + inv_std * inner).astype(BF16)
    gain = jnp.sum(normed_grad * normalized, axis=0, keepdims=True)
    high = gain.astype(BF16).astype(F32)
    middle = (gain - high).astype(BF16).astype(F32)
    row = lax.broadcasted_iota(jnp.int32, (16, D), 0)
    split = jnp.where(row == 2, gain - high - middle, 0.0)
    split = jnp.where(row == 0, high, jnp.where(row == 1, middle, split)).astype(BF16)
    blocks = []
    for block in range(4):
        rows = slice(block * 320, (block + 1) * 320)
        ordered = jnp.sum(dot(split, pick_ref[rows, :], NT), axis=0, keepdims=True)
        blocks.append(jnp.concatenate([ordered, jnp.zeros((1, 64), F32)], axis=1))
    even = (place_ref[1] & 1) == 0
    near = jnp.where(even, blocks[1], blocks[3])
    far = jnp.where(even, blocks[3], blocks[1])
    rest = jnp.zeros((6, 384), F32)
    keep[...] = jnp.concatenate([blocks[0], near, rest], axis=0)
    give[...] = jnp.concatenate([blocks[2], far, rest], axis=0)


def gain_body(keep, arrived, own, give):
    total = keep[...] + arrived[...]
    own[...] = total
    give[...] = jnp.concatenate([total[1:8], total[0:1]], axis=0)


def pick(source):
    lanes = lax.broadcasted_iota(jnp.int32, (source.shape[0], D), 1)
    return jnp.where(lanes == source, 1.0, 0.0).astype(BF16)


def relative_rows(place_ref, order, block):
    here = {"z": place_ref[0], "x": place_ref[1], "y": place_ref[2]}
    on_first = place_ref[3] == 0
    row = lax.broadcasted_iota(jnp.int32, (320, 1), 0)

    def count(value, size):
        return sum(jnp.where(value >= size * step, 1, 0) for step in (1, 2, 3))

    def offset(axis, at):
        if axis == "x":
            return (at & 1) * 160 + (at >> 1) * 80
        return at * (320 if axis == "z" else 20)

    second = count(row, 80)
    row = row - 80 * second
    third = count(row, 20)
    row = row - 20 * third
    for level, step in enumerate((block, second, third)):
        one, two = (
            offset(axes[level], (here[axes[level]] + step) & 3) for axes in order
        )
        row = row + jnp.where(on_first, one, two)
    return row


def ready_body(place_ref, pick_a, pick_b, pick_att, token):
    token[...] = jnp.zeros((8, 128), F32)
    for step in range(4):
        rows = slice(step * 320, (step + 1) * 320)
        pick_a[rows, :] = pick(relative_rows(place_ref, ORDER_A, step))
        feature = relative_rows(place_ref, ORDER_B, step)
        pick_b[rows, :] = pick(feature)
        feature = feature + place_ref[3] * HALF
        pick_att[rows, :] = pick(jnp.where(feature >= D, feature - D, feature))


def gained_body(pick_ref, own_ref, partner_ref, out):
    for step in range(4):
        rows = slice(step * 320, (step + 1) * 320)
        out[rows, :TOKENS] = dot(pick_ref[rows, :], own_ref[...], NT).astype(BF16)
        out[rows, TOKENS:] = dot(pick_ref[rows, :], partner_ref[...], NT).astype(BF16)


def turn_body(pick_att, mine, other, their_mine, theirs, att_out):
    sides = ((mine, other), (theirs, their_mine))
    for step in range(4):
        rows = slice(step * 320, (step + 1) * 320)
        for which, (first, second) in enumerate(sides):
            turned = dot(pick_att[rows, :HALF], first[:, :HALF], NT)
            turned += dot(pick_att[rows, HALF:], second[:, :HALF], NT)
            att_out[rows, which * TOKENS:(which + 1) * TOKENS] = turned.astype(BF16)


def term_a(rows, gained, stack, theirs):
    return dot(gained[rows, :TOKENS], stack[...]) + dot(gained[rows, TOKENS:], theirs[:, HALF:])


def term_b(rows, place_ref, both, their_cot, att):
    outer = dot(att[rows, :TOKENS], side(both, 1, half(place_ref, True)))
    return outer + dot(att[rows, TOKENS:], their_cot[...])


def early_body(term, count, *refs):
    plus, minus = refs[count:]
    far = term(slice(640, 960), *refs[:count])
    plus[0:160, :] = far[0:160].astype(BF16)
    minus[0:160, :] = far[160:320].astype(BF16)
    plus[160:320, :] = term(slice(480, 640), *refs[:count]).astype(BF16)
    minus[160:320, :] = term(slice(960, 1120), *refs[:count]).astype(BF16)


def relay_body(term, count, *refs):
    from_minus, from_plus, plus, minus = refs[count:]
    up = term(slice(320, 480), *refs[:count]) + from_minus[0:160, :].astype(F32)
    down = term(slice(1120, 1280), *refs[:count]) + from_plus[0:160, :].astype(F32)
    plus[...] = up.astype(BF16)
    minus[...] = down.astype(BF16)


def own_body(term, count, *refs):
    from_minus, from_plus, own = refs[count:]
    total = term(slice(0, 320), *refs[:count])
    own[0:160, :] = total[0:160] + from_plus[160:320, :].astype(F32)
    own[160:320, :] = total[160:320] + from_minus[160:320, :].astype(F32)


def second_early_body(own, from_minus, from_plus, *refs):
    gains, (rest, plus, minus) = refs[:-3], refs[-3:]
    upper = own[0:160, :] + from_minus[...].astype(F32)
    lower = own[160:320, :] + from_plus[...].astype(F32)
    if gains:
        line = gains[0][0:1, :] + gains[1][0:1, :]
        row = lax.broadcasted_iota(jnp.int32, (320, 384), 0)
        lane = lax.broadcasted_iota(jnp.int32, (320, 384), 1)
        column = jnp.sum(jnp.where(row == lane, line, 0.0), axis=-1, keepdims=True)
        column = jnp.where(lane[:, :128] == 0, column, 0.0)
        upper = jnp.concatenate([upper, column[0:160]], axis=1)
        lower = jnp.concatenate([lower, column[160:320]], axis=1)
    rest[0:120, :] = upper[0:120]
    plus[40:80, :] = upper[120:160]
    plus[0:40, :] = lower[0:40]
    minus[0:80, :] = lower[40:120]
    rest[120:160, :] = lower[120:160]


def second_relay_body(rest, from_minus, from_plus, plus, minus, part):
    plus[...] = rest[80:120, :] + from_minus[0:40, :]
    minus[...] = rest[120:160, :] + from_plus[0:40, :]
    part[0:40, :] = rest[0:40, :] + from_plus[40:80, :]
    part[40:80, :] = rest[40:80, :] + from_minus[40:80, :]


def third_body(part, last_minus, last_plus, own, one, two, three):
    upper = part[0:40, :] + last_minus[...]
    lower = part[40:80, :] + last_plus[...]
    own[...] = upper[0:20]
    one[...] = upper[20:40]
    two[...] = lower[0:20]
    three[...] = lower[20:40]


def add_body(own, one, two, three, out):
    out[...] = (own[...] + one[...]) + (two[...] + three[...])


def final_body(place_ref, total_a, own, one, two, three, here, other):
    on_first = place_ref[3] == 0
    total_b = (own[...] + one[...]) + (two[...] + three[...])
    total = jnp.concatenate([total_a[...], total_b], axis=1)
    low, high = total[0:10], total[10:20]
    here[...] = jnp.where(on_first, low, high)
    other[...] = jnp.where(on_first, high, low)


def assemble_body(place_ref, here, theirs, qkv_ref, out_ref, gain_ref):
    first = place_ref[3] == 0
    left = jnp.where(first, here[...], theirs[...]) * FACTOR
    right = jnp.where(first, theirs[...], here[...]) * FACTOR
    for which, value in enumerate((left, right)):
        out_ref[:, which * HALF:(which + 1) * HALF] = value[:, WIDTH_A:WIDTH_A + HALF]
        for part in range(3):
            at = part * D + which * HALF
            qkv_ref[:, at:at + HALF] = value[:, part * HALF:(part + 1) * HALF]
    both = left[:, WIDTH_A + HALF:] + right[:, WIDTH_A + HALF:]
    column = jnp.sum(both, axis=-1, keepdims=True)
    row = lax.broadcasted_iota(jnp.int32, (10, 10), 0)
    lane = lax.broadcasted_iota(jnp.int32, (10, 10), 1)
    gain_ref[...] = jnp.sum(jnp.where(row == lane, column, 0.0), axis=0, keepdims=True)


def send(value, order, level, step):
    pairs = []
    for source in range(128):
        spots = {
            "z": source // 32, "x": source // 16 % 2 + source // 8 % 2 * 2, "y": source // 2 % 4
        }
        axis = order[source % 2][level]
        spots[axis] = (spots[axis] + step) % 4
        column = spots["x"] % 2 * 2 + spots["x"] // 2
        target = ((spots["z"] * 4 + column) * 4 + spots["y"]) * 2 + source % 2
        pairs.append((source, target))
    return lax.ppermute(value, ("z", "xl", "xh", "y", "c"), pairs)


def swap(value):
    return lax.ppermute(value, "c", [(0, 1), (1, 0)])


def split_body(x_ref, cot_ref, out_ref, sems):
    copies = [
        pltpu.make_async_copy(value.at[frame], out_ref.at[:, which, frame], sems.at[which, frame])
        for which, value in enumerate((x_ref, cot_ref))
        for frame in range(4)
    ]
    for copy in copies:
        copy.start()
    for copy in copies:
        copy.wait()


def join_body(value_ref, after_ref, out_ref, token_ref, sems):
    copies = [
        pltpu.make_async_copy(value_ref.at[:, frame], out_ref.at[frame], sems.at[frame])
        for frame in range(4)
    ]
    for copy in copies:
        copy.start()
    token_ref[...] = after_ref[...]
    for copy in copies:
        copy.wait()


def on_device(activations, grad_out, norm_gain, qkv_weight, out_weight):
    anywhere = pl.BlockSpec(memory_space=pl.ANY)
    in_vmem = pl.BlockSpec(memory_space=pltpu.VMEM)
    params = pltpu.CompilerParams(vmem_limit_bytes=16 * 2**20)
    x_place = lax.axis_index("xh") * 2 + lax.axis_index("xl")
    place = jnp.stack([lax.axis_index("z"), x_place, lax.axis_index("y"), lax.axis_index("c")])
    place = place.astype(jnp.int32)
    group = place[3:]
    gain_row = norm_gain.reshape(1, D)
    both = pl.pallas_call(
        split_body, out_shape=pltpu.VMEM((8, 2, 4, 8, D), BF16), in_specs=[anywhere] * 2,
        out_specs=in_vmem, scratch_shapes=[pltpu.SemaphoreType.DMA((2, 4))],
        compiler_params=params,
    )(from_hbm(activations.reshape(4, 8, 8, D)), from_hbm(grad_out.reshape(4, 8, 8, D)))
    pick_a, pick_b, pick_att, token = pl.pallas_call(
        ready_body, out_shape=[pltpu.HBM((D, D), BF16)] * 3 + [shape(8, 128, F32)],
        in_specs=[pl.BlockSpec(memory_space=pltpu.SMEM)], out_specs=[in_vmem] * 4,
        compiler_params=params,
        cost_estimate=pl.CostEstimate(flops=10**9, bytes_accessed=2 * 10**7, transcendentals=0),
    )(place)
    both = lax.all_to_all(both, ("z", "xl"), split_axis=0, concat_axis=0, tiled=True)
    both = both.reshape(8, 64, D)
    (gained, qkv, cot_other, weight, hat, inv_std, held_out), token = call(
        forward_body,
        [shape(TOKENS, D), shape(TOKENS, 3 * D), shape(TOKENS, HALF), shape(D, 3 * D),
         shape(TOKENS, D, F32), shape(TOKENS, 128, F32), shape(D, D)],
        [place, both, gain_row, qkv_weight, out_weight], scalars=1, flops=2 * TOKENS * D * 3 * D,
        scratch=[pltpu.SemaphoreType.DMA((7,))], hbm=(3, 4), after=[token],
    )
    their_gained, their_cot = swap(gained), swap(cot_other)

    def attention(which, after, outs):
        return call(
            attention_body if len(outs) == 2 else joint_attention_body, outs,
            [which, qkv, both, held_out], scalars=1, flops=5 * 10**9,
            scratch=[pltpu.VMEM((TOKENS, HALF), BF16), pltpu.VMEM((TOKENS, TOKENS), F32)],
            after=after,
        )

    (other_half,), token = attention(1 - group, token, [shape(TOKENS, 4 * HALF)])
    their_half = swap(other_half)
    (att_mine, stack), token = attention(
        group, token, [shape(TOKENS, HALF), shape(TOKENS, 3 * HALF)]
    )
    their_mine = swap(att_mine)
    (gained_a,), token = call(
        gained_body, [shape(D, 512)], [pick_a, gained, their_gained], flops=2 * D * D * 512,
        after=token,
    )
    work = {"a": 10**7, "b": 15 * 10**8, "b second": 8 * 10**9}
    base = {"a": [gained_a, stack, their_half]}
    kinds = {"a": (term_a, 0, WIDTH_A, ORDER_A), "b": (term_b, 1, HALF, ORDER_B)}

    def run(which, body, outs, extra, after):
        term, scalars, _, _ = kinds[which]
        return call(
            functools.partial(body, term, len(base[which])), outs, base[which] + extra,
            scalars=scalars, flops=work[which], after=after,
        )

    def exchange(which, sent, level):
        order = kinds[which][3]
        return [send(sent[0], order, level, 1), send(sent[1], order, level, 3)]

    state = {}

    def early(which, after):
        sent, after = run(which, early_body, [shape(320, kinds[which][2])] * 2, [], after)
        state[which] = exchange(which, sent, 0)
        return after

    def relay(which, after):
        width, first = kinds[which][2], state[which]
        sent, after = run(which, relay_body, [shape(160, width)] * 2, first, after)
        state[which] = (first, exchange(which, sent, 0))
        return after

    def own_rows(which, after):
        first, second = state[which]
        outs = [shape(320, kinds[which][2], F32)]
        own, after = run(which, own_body, outs, first, after)
        state[which] = own + second
        return after

    gains = {"a": [], "b": []}

    def second_early(which, after):
        width = kinds[which][2] + (128 if gains[which] else 0)
        outs = [shape(rows, width, F32) for rows in (160, 80, 80)]
        (rest, *sent), after = call(
            second_early_body, outs, state[which] + gains[which], after=after,
            flops=work["b second" if which == "b" else "a"],
        )
        state[which] = [rest] + exchange(which, sent, 1)
        return after

    def second_relay(which, after):
        width = state[which][0].shape[1]
        outs = [shape(40, width, F32)] * 2 + [shape(80, width, F32)]
        (plus, minus, part), after = call(
            second_relay_body, outs, state[which], flops=work[which], after=after
        )
        state[which] = [part] + exchange(which, (plus, minus), 1)
        return after

    def third(which, after):
        outs = [shape(20, state[which][0].shape[1], F32)] * 4
        (own, *others), after = call(
            third_body, outs, state[which], flops=work[which], after=after
        )
        order = kinds[which][3]
        sent = [send(other, order, 2, step + 1) for step, other in enumerate(others)]
        state[which] = [own] + sent
        return after

    token = early("a", token + [their_mine])
    (att,), token = call(
        turn_body, [shape(D, 512)], [pick_att, att_mine, other_half, their_mine, their_half],
        after=token,
    )
    base["b"] = [place, both, their_cot, att]
    token = early("b", token)
    (grad_here, keep, give), token = call(
        input_grad_body, [shape(TOKENS, D)] + [shape(8, 384, F32)] * 2,
        [place, both, hat, inv_std, gain_row, weight, stack, other_half, pick_b], scalars=1,
        after=token,
        scratch=[pltpu.VMEM((TOKENS, 3 * D), BF16)],
    )
    arrived = lax.ppermute(give, "xh", [(0, 1), (1, 0)])
    token = relay("b", relay("a", token))
    token = own_rows("b", own_rows("a", token))
    (own, give), token = call(gain_body, [shape(8, 384, F32)] * 2, [keep, arrived], after=token)
    gains["b"] = [own, lax.ppermute(give, "xl", [(0, 1), (1, 0)])]
    token = second_early("b", second_early("a", token))
    grad_here, token = late(grad_here, token)
    back = lax.all_to_all(
        grad_here.reshape(8, 4, 8, D), ("z", "xl"), split_axis=0, concat_axis=0, tiled=True
    )
    token = second_relay("b", second_relay("a", token))
    token = third("b", third("a", token))
    (total_a,), token = call(add_body, [shape(20, WIDTH_A, F32)], state["a"], after=token)
    grad_tokens, token = pl.pallas_call(
        join_body,
        out_shape=[jax.ShapeDtypeStruct((4, 8, 8, D), BF16), pltpu.VMEM((8, 128), F32)],
        in_specs=[anywhere, in_vmem], out_specs=[anywhere, in_vmem],
        scratch_shapes=[pltpu.SemaphoreType.DMA((4,))], compiler_params=params,
        cost_estimate=pl.CostEstimate(flops=10**7, bytes_accessed=1, transcendentals=0),
    )(back, pltpu.with_memory_space_constraint(token[0], pltpu.VMEM))
    (here, other), token = call(
        final_body, [shape(10, WIDTH_A + WIDTH_B, F32)] * 2, [place, total_a] + state["b"],
        scalars=1, after=[token],
    )
    theirs = swap(other)
    (qkv_grad, out_grad, gain_grad), _ = call(
        assemble_body, [shape(10, 3 * D, F32), shape(10, D, F32), shape(1, 10, F32)],
        [place, here, theirs], scalars=1, results=jax.ShapeDtypeStruct, last=True,
        after=token,
    )
    return (grad_tokens.reshape(1, 4, 64, D), qkv_grad, out_grad, gain_grad.reshape(10))


def solution(mesh):
    fine = Mesh(mesh.devices.reshape(4, 2, 2, 4, 2), ("z", "xl", "xh", "y", "c"))
    tm, space = ("z", "xl"), ("xh", "y", "c")
    tokens = P(None, tm, space, None)
    in_specs = (tokens, tokens, P(), P(), P())
    out_specs = (tokens, P(tm + space, None), P(tm + space, None), P(tm + space))
    return jax.shard_map(
        on_device, mesh=fine, in_specs=in_specs, out_specs=out_specs, check_vma=False
    )
```

```python
import functools
import math

import jax
import jax.numpy as jnp
from jax import lax
from jax.experimental import pallas as pl
from jax.experimental.pallas import tpu as pltpu
from jax.sharding import Mesh, PartitionSpec as P

D = 1280
HEADS = 16
HEAD = 80
HALF = 640
TOKENS = 256
INVERSE_ROOT = 1.0 / math.sqrt(HEAD)
FACTOR = 1.0 / math.sqrt(32 * 1024)
BF16, F32 = jnp.bfloat16, jnp.float32
ORDER_A = (("z", "y", "x"), ("y", "x", "z"))
ORDER_B = (("x", "y", "z"), ("x", "z", "y"))
WIDTH_A, WIDTH_B = 1920, 768
NN = (((1,), (0,)), ((), ()))
NT = (((1,), (1,)), ((), ()))
TN = (((0,), (0,)), ((), ()))


def dot(left, right, dims=NN):
    return lax.dot_general(left, right, dims, preferred_element_type=F32)


def call(body, outs, operands, scalars=0, flops=0, scratch=(), after=None, results=pltpu.VMEM,
         hbm=(), last=False):
    vmem = pl.BlockSpec(memory_space=pltpu.VMEM)
    smem = pl.BlockSpec(memory_space=pltpu.SMEM)
    count, tokens = len(operands), [] if last else [pltpu.VMEM((8, 128), F32)]
    size = sum(math.prod(o.shape) * o.dtype.itemsize for o in list(operands) + list(outs))
    given = list(operands) + ([] if after is None else list(after))
    spaces = [smem] * scalars + [vmem] * (len(given) - scalars)
    placed = [
        value if place < scalars else pltpu.with_memory_space_constraint(value, pltpu.VMEM)
        for place, value in enumerate(given)
    ]
    for place in hbm:
        spaces[place] = pl.BlockSpec(memory_space=pl.ANY)
        placed[place] = from_hbm(given[place])

    def run(*refs):
        results, rest = refs[len(placed):len(placed) + len(outs)], refs[len(placed) + len(outs):]
        if not last:
            rest[0][...] = jnp.zeros((8, 128), F32)
            rest = rest[1:]
        body(*refs[:count], *results, *rest)

    given = pl.pallas_call(
        run,
        out_shape=[results(o.shape, o.dtype) for o in outs] + tokens,
        in_specs=spaces,
        out_specs=[vmem] * (len(outs) + len(tokens)),
        scratch_shapes=scratch,
        compiler_params=pltpu.CompilerParams(vmem_limit_bytes=16 * 2**20),
        cost_estimate=pl.CostEstimate(
            flops=flops, bytes_accessed=size // 4 if flops else 1, transcendentals=0
        ),
    )(*placed)
    return list(given[:len(outs)]), list(given[len(outs):])


def late(value, after):
    vmem, anywhere = pl.BlockSpec(memory_space=pltpu.VMEM), pl.BlockSpec(memory_space=pl.ANY)

    def body(*refs):
        refs[-1][...] = jnp.zeros((8, 128), F32)

    value, token = pl.pallas_call(
        body,
        out_shape=[jax.ShapeDtypeStruct(value.shape, value.dtype), pltpu.VMEM((8, 128), F32)],
        in_specs=[anywhere] + [vmem] * len(after), out_specs=[anywhere, vmem],
        input_output_aliases={0: 0},
        compiler_params=pltpu.CompilerParams(vmem_limit_bytes=2**20),
        cost_estimate=pl.CostEstimate(flops=10**7, bytes_accessed=1, transcendentals=0),
    )(value, *[pltpu.with_memory_space_constraint(array, pltpu.VMEM) for array in after])
    return value, [token]


def from_hbm(value):
    return pltpu.with_memory_space_constraint(value, pltpu.HBM)


def shape(rows, columns, kind=BF16):
    return jax.ShapeDtypeStruct((rows, columns), kind)


def side(both_ref, which, columns=slice(None)):
    value = both_ref[:, 32 * which:32 * which + 32, columns]
    return value.reshape(TOKENS, value.shape[-1])


def normalize(both_ref):
    x_wide = side(both_ref, 0).astype(F32)
    centred = x_wide - jnp.mean(x_wide, axis=-1, keepdims=True)
    variance = jnp.mean(centred * centred, axis=-1, keepdims=True)
    inv_std = lax.rsqrt(variance + 1e-06)
    return centred * inv_std, inv_std


def half(place_ref, own):
    core = place_ref[3] if own else 1 - place_ref[3]
    return pl.ds(pl.multiple_of(core * HALF, 128), HALF)


def forward_body(place_ref, both_ref, gain_ref, weight_ref, out_weight_ref, gained_ref, qkv_ref, cot_ref,
                 held_ref, hat_ref, inv_ref, out_held_ref, sems):
    pieces = [slice(step * HALF, (step + 1) * HALF) for step in range(6)]
    copies = [
        pltpu.make_async_copy(weight_ref.at[:, piece], held_ref.at[:, piece], sems.at[step])
        for step, piece in enumerate(pieces)
    ]
    copies.append(pltpu.make_async_copy(out_weight_ref, out_held_ref, sems.at[6]))
    for copy in copies[:3]:
        copy.start()
    normalized, inv_std = normalize(both_ref)
    hat_ref[...] = normalized
    inv_ref[...] = jnp.broadcast_to(inv_std, (TOKENS, 128))
    gained = (normalized * gain_ref[...]).astype(BF16)
    gained_ref[...] = gained
    cot_ref[...] = side(both_ref, 1, half(place_ref, False))
    for step, (copy, piece) in enumerate(zip(copies, pieces)):
        copy.wait()
        if step + 3 < len(copies):
            copies[step + 3].start()
        qkv_ref[:, piece] = dot(gained, held_ref[:, piece]).astype(BF16)
    copies[6].wait()


def attention_body(group_ref, qkv_ref, both_ref, weight_ref, att_ref, stack_ref, ag_ref,
                   bias_ref):
    start = pl.multiple_of(group_ref[0] * HALF, 128)
    ag_ref[...] = dot(side(both_ref, 1), weight_ref[pl.ds(start, HALF), :], NT).astype(BF16)
    row = lax.broadcasted_iota(jnp.int32, (TOKENS, TOKENS), 0)
    column = lax.broadcasted_iota(jnp.int32, (TOKENS, TOKENS), 1)
    bias_ref[...] = jnp.where((row & 7) == (column & 7), 0.0, -1e30)
    tiles = [[[] for _ in range(5)] for _ in range(4)]
    for head in range(8):
        low, high = head * HEAD, (head + 1) * HEAD
        first, last = low // 128 * 128, -(-high // 128) * 128
        width = last - first
        lanes = lax.broadcasted_iota(jnp.int32, (1, width), 1) + first
        keep = jnp.where((lanes >= low) & (lanes < high), 1.0, 0.0).astype(BF16)

        def cut(part):
            return qkv_ref[:, pl.ds(pl.multiple_of(start + part * D + first, 128), width)] * keep

        query, key, value = cut(0), cut(1), cut(2)
        grad = ag_ref[:, first:last] * keep
        scores = dot(key, query, NT) + bias_ref[...]
        shifted = jnp.exp((scores - jnp.max(scores, axis=0, keepdims=True)) * INVERSE_ROOT)
        prob = shifted * (1.0 / jnp.sum(shifted, axis=0, keepdims=True))
        prob_low = prob.astype(BF16)
        prob_grad = dot(value, grad, NT)
        mixed = jnp.sum(prob_grad * prob, axis=0, keepdims=True)
        score_grad = (prob * (prob_grad - mixed) * INVERSE_ROOT).astype(BF16)
        results = (
            dot(prob_low, value, TN), dot(score_grad, key, TN), dot(score_grad, query),
            dot(prob_low, grad),
        )
        for kind, result in enumerate(results):
            for tile in range(width // 128):
                piece = result[:, tile * 128:(tile + 1) * 128]
                tiles[kind][first // 128 + tile].append(piece)
    for kind in range(4):
        for tile in range(5):
            total = sum(tiles[kind][tile][1:], tiles[kind][tile][0]).astype(BF16)
            if kind == 0:
                att_ref[:, tile * 128:(tile + 1) * 128] = total
            else:
                at = (kind - 1) * HALF + tile * 128
                stack_ref[:, at:at + 128] = total


def joint_attention_body(group_ref, qkv_ref, both_ref, weight_ref, out_ref, *scratch):
    attention_body(
        group_ref, qkv_ref, both_ref, weight_ref, out_ref.at[:, :HALF], out_ref.at[:, HALF:],
        *scratch
    )


def input_grad_body(place_ref, both_ref, hat_ref, inv_ref, gain_ref, weight_ref, mine_ref,
                    other_ref, pick_ref,
                    grad_ref, keep, give, joined_ref):
    for own, stack_ref in ((True, mine_ref), (False, other_ref)):
        group = place_ref[3] if own else 1 - place_ref[3]
        for part in range(3):
            columns = pl.ds(pl.multiple_of(group * HALF + part * D, 128), HALF)
            start = part * HALF if own else (part + 1) * HALF
            joined_ref[:, columns] = stack_ref[:, start:start + HALF]
    normed_grad = dot(joined_ref[...], weight_ref[...], NT)
    normalized, inv_std = hat_ref[...], inv_ref[:, 0:1]
    scaled = normed_grad * gain_ref[...]
    inner = scaled - jnp.mean(scaled, axis=-1, keepdims=True)
    inner -= normalized * jnp.mean(scaled * normalized, axis=-1, keepdims=True)
    grad_ref[...] = (side(both_ref, 1).astype(F32) + inv_std * inner).astype(BF16)
    gain = jnp.sum(normed_grad * normalized, axis=0, keepdims=True)
    high = gain.astype(BF16).astype(F32)
    middle = (gain - high).astype(BF16).astype(F32)
    row = lax.broadcasted_iota(jnp.int32, (16, D), 0)
    split = jnp.where(row == 2, gain - high - middle, 0.0)
    split = jnp.where(row == 0, high, jnp.where(row == 1, middle, split)).astype(BF16)
    blocks = []
    for block in range(4):
        rows = slice(block * 320, (block + 1) * 320)
        ordered = jnp.sum(dot(split, pick_ref[rows, :], NT), axis=0, keepdims=True)
        blocks.append(jnp.concatenate([ordered, jnp.zeros((1, 64), F32)], axis=1))
    even = (place_ref[1] & 1) == 0
    near = jnp.where(even, blocks[1], blocks[3])
    far = jnp.where(even, blocks[3], blocks[1])
    rest = jnp.zeros((6, 384), F32)
    keep[...] = jnp.concatenate([blocks[0], near, rest], axis=0)
    give[...] = jnp.concatenate([blocks[2], far, rest], axis=0)


def gain_body(keep, arrived, own, give):
    total = keep[...] + arrived[...]
    own[...] = total
    give[...] = jnp.concatenate([total[1:8], total[0:1]], axis=0)


def pick(source):
    lanes = lax.broadcasted_iota(jnp.int32, (source.shape[0], D), 1)
    return jnp.where(lanes == source, 1.0, 0.0).astype(BF16)


def relative_rows(place_ref, order, block):
    here = {"z": place_ref[0], "x": place_ref[1], "y": place_ref[2]}
    on_first = place_ref[3] == 0
    row = lax.broadcasted_iota(jnp.int32, (320, 1), 0)

    def count(value, size):
        return sum(jnp.where(value >= size * step, 1, 0) for step in (1, 2, 3))

    def offset(axis, at):
        if axis == "x":
            return (at & 1) * 160 + (at >> 1) * 80
        return at * (320 if axis == "z" else 20)

    second = count(row, 80)
    row = row - 80 * second
    third = count(row, 20)
    row = row - 20 * third
    for level, step in enumerate((block, second, third)):
        one, two = (
            offset(axes[level], (here[axes[level]] + step) & 3) for axes in order
        )
        row = row + jnp.where(on_first, one, two)
    return row


def ready_body(place_ref, pick_a, pick_b, pick_att, token):
    token[...] = jnp.zeros((8, 128), F32)
    for step in range(4):
        rows = slice(step * 320, (step + 1) * 320)
        pick_a[rows, :] = pick(relative_rows(place_ref, ORDER_A, step))
        feature = relative_rows(place_ref, ORDER_B, step)
        pick_b[rows, :] = pick(feature)
        feature = feature + place_ref[3] * HALF
        pick_att[rows, :] = pick(jnp.where(feature >= D, feature - D, feature))


def gained_body(pick_ref, own_ref, partner_ref, out):
    for step in range(4):
        rows = slice(step * 320, (step + 1) * 320)
        out[rows, :TOKENS] = dot(pick_ref[rows, :], own_ref[...], NT).astype(BF16)
        out[rows, TOKENS:] = dot(pick_ref[rows, :], partner_ref[...], NT).astype(BF16)


def turn_body(pick_att, mine, other, their_mine, theirs, att_out):
    sides = ((mine, other), (theirs, their_mine))
    for step in range(4):
        rows = slice(step * 320, (step + 1) * 320)
        for which, (first, second) in enumerate(sides):
            turned = dot(pick_att[rows, :HALF], first[:, :HALF], NT)
            turned += dot(pick_att[rows, HALF:], second[:, :HALF], NT)
            att_out[rows, which * TOKENS:(which + 1) * TOKENS] = turned.astype(BF16)


def term_a(rows, gained, stack, theirs):
    return dot(gained[rows, :TOKENS], stack[...]) + dot(gained[rows, TOKENS:], theirs[:, HALF:])


def term_b(rows, place_ref, both, their_cot, att):
    outer = dot(att[rows, :TOKENS], side(both, 1, half(place_ref, True)))
    return outer + dot(att[rows, TOKENS:], their_cot[...])


def early_body(term, count, *refs):
    plus, minus = refs[count:]
    far = term(slice(640, 960), *refs[:count])
    plus[0:160, :] = far[0:160].astype(BF16)
    minus[0:160, :] = far[160:320].astype(BF16)
    plus[160:320, :] = term(slice(480, 640), *refs[:count]).astype(BF16)
    minus[160:320, :] = term(slice(960, 1120), *refs[:count]).astype(BF16)


def relay_body(term, count, *refs):
    from_minus, from_plus, plus, minus = refs[count:]
    up = term(slice(320, 480), *refs[:count]) + from_minus[0:160, :].astype(F32)
    down = term(slice(1120, 1280), *refs[:count]) + from_plus[0:160, :].astype(F32)
    plus[...] = up.astype(BF16)
    minus[...] = down.astype(BF16)


def own_body(term, count, *refs):
    from_minus, from_plus, own = refs[count:]
    total = term(slice(0, 320), *refs[:count])
    own[0:160, :] = total[0:160] + from_plus[160:320, :].astype(F32)
    own[160:320, :] = total[160:320] + from_minus[160:320, :].astype(F32)


def second_early_body(own, from_minus, from_plus, *refs):
    gains, (rest, plus, minus) = refs[:-3], refs[-3:]
    upper = own[0:160, :] + from_minus[...].astype(F32)
    lower = own[160:320, :] + from_plus[...].astype(F32)
    if gains:
        line = gains[0][0:1, :] + gains[1][0:1, :]
        row = lax.broadcasted_iota(jnp.int32, (320, 384), 0)
        lane = lax.broadcasted_iota(jnp.int32, (320, 384), 1)
        column = jnp.sum(jnp.where(row == lane, line, 0.0), axis=-1, keepdims=True)
        column = jnp.where(lane[:, :128] == 0, column, 0.0)
        upper = jnp.concatenate([upper, column[0:160]], axis=1)
        lower = jnp.concatenate([lower, column[160:320]], axis=1)
    rest[0:120, :] = upper[0:120]
    plus[40:80, :] = upper[120:160]
    plus[0:40, :] = lower[0:40]
    minus[0:80, :] = lower[40:120]
    rest[120:160, :] = lower[120:160]


def second_relay_body(rest, from_minus, from_plus, plus, minus, part):
    plus[...] = rest[80:120, :] + from_minus[0:40, :]
    minus[...] = rest[120:160, :] + from_plus[0:40, :]
    part[0:40, :] = rest[0:40, :] + from_plus[40:80, :]
    part[40:80, :] = rest[40:80, :] + from_minus[40:80, :]


def third_body(part, last_minus, last_plus, own, one, two, three):
    upper = part[0:40, :] + last_minus[...]
    lower = part[40:80, :] + last_plus[...]
    own[...] = upper[0:20]
    one[...] = upper[20:40]
    two[...] = lower[0:20]
    three[...] = lower[20:40]


def add_body(own, one, two, three, out):
    out[...] = (own[...] + one[...]) + (two[...] + three[...])


def final_body(place_ref, total_a, own, one, two, three, here, other):
    on_first = place_ref[3] == 0
    total_b = (own[...] + one[...]) + (two[...] + three[...])
    total = jnp.concatenate([total_a[...], total_b], axis=1)
    low, high = total[0:10], total[10:20]
    here[...] = jnp.where(on_first, low, high)
    other[...] = jnp.where(on_first, high, low)


def assemble_body(place_ref, here, theirs, qkv_ref, out_ref, gain_ref):
    first = place_ref[3] == 0
    left = jnp.where(first, here[...], theirs[...]) * FACTOR
    right = jnp.where(first, theirs[...], here[...]) * FACTOR
    for which, value in enumerate((left, right)):
        out_ref[:, which * HALF:(which + 1) * HALF] = value[:, WIDTH_A:WIDTH_A + HALF]
        for part in range(3):
            at = part * D + which * HALF
            qkv_ref[:, at:at + HALF] = value[:, part * HALF:(part + 1) * HALF]
    both = left[:, WIDTH_A + HALF:] + right[:, WIDTH_A + HALF:]
    column = jnp.sum(both, axis=-1, keepdims=True)
    row = lax.broadcasted_iota(jnp.int32, (10, 10), 0)
    lane = lax.broadcasted_iota(jnp.int32, (10, 10), 1)
    gain_ref[...] = jnp.sum(jnp.where(row == lane, column, 0.0), axis=0, keepdims=True)


def send(value, order, level, step):
    pairs = []
    for source in range(128):
        spots = {
            "z": source // 32, "x": source // 16 % 2 + source // 8 % 2 * 2, "y": source // 2 % 4
        }
        axis = order[source % 2][level]
        spots[axis] = (spots[axis] + step) % 4
        column = spots["x"] % 2 * 2 + spots["x"] // 2
        target = ((spots["z"] * 4 + column) * 4 + spots["y"]) * 2 + source % 2
        pairs.append((source, target))
    return lax.ppermute(value, ("z", "xl", "xh", "y", "c"), pairs)


def swap(value):
    return lax.ppermute(value, "c", [(0, 1), (1, 0)])


def split_body(x_ref, cot_ref, out_ref, sems):
    copies = [
        pltpu.make_async_copy(value.at[frame], out_ref.at[:, which, frame], sems.at[which, frame])
        for which, value in enumerate((x_ref, cot_ref))
        for frame in range(4)
    ]
    for copy in copies:
        copy.start()
    for copy in copies:
        copy.wait()


def join_body(value_ref, after_ref, out_ref, token_ref, sems):
    copies = [
        pltpu.make_async_copy(value_ref.at[:, frame], out_ref.at[frame], sems.at[frame])
        for frame in range(4)
    ]
    for copy in copies:
        copy.start()
    token_ref[...] = after_ref[...]
    for copy in copies:
        copy.wait()


def on_device(activations, grad_out, norm_gain, qkv_weight, out_weight):
    anywhere = pl.BlockSpec(memory_space=pl.ANY)
    in_vmem = pl.BlockSpec(memory_space=pltpu.VMEM)
    params = pltpu.CompilerParams(vmem_limit_bytes=16 * 2**20)
    x_place = lax.axis_index("xh") * 2 + lax.axis_index("xl")
    place = jnp.stack([lax.axis_index("z"), x_place, lax.axis_index("y"), lax.axis_index("c")])
    place = place.astype(jnp.int32)
    group = place[3:]
    gain_row = norm_gain.reshape(1, D)
    both = pl.pallas_call(
        split_body, out_shape=pltpu.VMEM((8, 2, 4, 8, D), BF16), in_specs=[anywhere] * 2,
        out_specs=in_vmem, scratch_shapes=[pltpu.SemaphoreType.DMA((2, 4))],
        compiler_params=params,
    )(from_hbm(activations.reshape(4, 8, 8, D)), from_hbm(grad_out.reshape(4, 8, 8, D)))
    pick_a, pick_b, pick_att, token = pl.pallas_call(
        ready_body, out_shape=[pltpu.HBM((D, D), BF16)] * 3 + [shape(8, 128, F32)],
        in_specs=[pl.BlockSpec(memory_space=pltpu.SMEM)], out_specs=[in_vmem] * 4,
        compiler_params=params,
        cost_estimate=pl.CostEstimate(flops=10**9, bytes_accessed=2 * 10**7, transcendentals=0),
    )(place)
    both = lax.all_to_all(both, ("z", "xl"), split_axis=0, concat_axis=0, tiled=True)
    both = both.reshape(8, 64, D)
    (gained, qkv, cot_other, weight, hat, inv_std, held_out), token = call(
        forward_body,
        [shape(TOKENS, D), shape(TOKENS, 3 * D), shape(TOKENS, HALF), shape(D, 3 * D),
         shape(TOKENS, D, F32), shape(TOKENS, 128, F32), shape(D, D)],
        [place, both, gain_row, qkv_weight, out_weight], scalars=1, flops=2 * TOKENS * D * 3 * D,
        scratch=[pltpu.SemaphoreType.DMA((7,))], hbm=(3, 4), after=[token],
    )
    their_gained, their_cot = swap(gained), swap(cot_other)

    def attention(which, after, outs):
        return call(
            attention_body if len(outs) == 2 else joint_attention_body, outs,
            [which, qkv, both, held_out], scalars=1, flops=5 * 10**9,
            scratch=[pltpu.VMEM((TOKENS, HALF), BF16), pltpu.VMEM((TOKENS, TOKENS), F32)],
            after=after,
        )

    (other_half,), token = attention(1 - group, token, [shape(TOKENS, 4 * HALF)])
    their_half = swap(other_half)
    (att_mine, stack), token = attention(
        group, token, [shape(TOKENS, HALF), shape(TOKENS, 3 * HALF)]
    )
    their_mine = swap(att_mine)
    (gained_a,), token = call(
        gained_body, [shape(D, 512)], [pick_a, gained, their_gained], flops=2 * D * D * 512,
        after=token,
    )
    work = {"a": 10**7, "b": 15 * 10**8, "b second": 8 * 10**9}
    base = {"a": [gained_a, stack, their_half]}
    kinds = {"a": (term_a, 0, WIDTH_A, ORDER_A), "b": (term_b, 1, HALF, ORDER_B)}

    def run(which, body, outs, extra, after):
        term, scalars, _, _ = kinds[which]
        return call(
            functools.partial(body, term, len(base[which])), outs, base[which] + extra,
            scalars=scalars, flops=work[which], after=after,
        )

    def exchange(which, sent, level):
        order = kinds[which][3]
        return [send(sent[0], order, level, 1), send(sent[1], order, level, 3)]

    state = {}

    def early(which, after):
        sent, after = run(which, early_body, [shape(320, kinds[which][2])] * 2, [], after)
        state[which] = exchange(which, sent, 0)
        return after

    def relay(which, after):
        width, first = kinds[which][2], state[which]
        sent, after = run(which, relay_body, [shape(160, width)] * 2, first, after)
        state[which] = (first, exchange(which, sent, 0))
        return after

    def own_rows(which, after):
        first, second = state[which]
        outs = [shape(320, kinds[which][2], F32)]
        own, after = run(which, own_body, outs, first, after)
        state[which] = own + second
        return after

    gains = {"a": [], "b": []}

    def second_early(which, after):
        width = kinds[which][2] + (128 if gains[which] else 0)
        outs = [shape(rows, width, F32) for rows in (160, 80, 80)]
        (rest, *sent), after = call(
            second_early_body, outs, state[which] + gains[which], after=after,
            flops=work["b second" if which == "b" else "a"],
        )
        state[which] = [rest] + exchange(which, sent, 1)
        return after

    def second_relay(which, after):
        width = state[which][0].shape[1]
        outs = [shape(40, width, F32)] * 2 + [shape(80, width, F32)]
        (plus, minus, part), after = call(
            second_relay_body, outs, state[which], flops=work[which], after=after
        )
        state[which] = [part] + exchange(which, (plus, minus), 1)
        return after

    def third(which, after):
        outs = [shape(20, state[which][0].shape[1], F32)] * 4
        (own, *others), after = call(
            third_body, outs, state[which], flops=work[which], after=after
        )
        order = kinds[which][3]
        sent = [send(other, order, 2, step + 1) for step, other in enumerate(others)]
        state[which] = [own] + sent
        return after

    token = early("a", token + [their_mine])
    (att,), token = call(
        turn_body, [shape(D, 512)], [pick_att, att_mine, other_half, their_mine, their_half],
        after=token,
    )
    base["b"] = [place, both, their_cot, att]
    token = early("b", token)
    (grad_here, keep, give), token = call(
        input_grad_body, [shape(TOKENS, D)] + [shape(8, 384, F32)] * 2,
        [place, both, hat, inv_std, gain_row, weight, stack, other_half, pick_b], scalars=1,
        after=token,
        scratch=[pltpu.VMEM((TOKENS, 3 * D), BF16)],
    )
    arrived = lax.ppermute(give, "xh", [(0, 1), (1, 0)])
    token = relay("b", relay("a", token))
    token = own_rows("b", own_rows("a", token))
    (own, give), token = call(gain_body, [shape(8, 384, F32)] * 2, [keep, arrived], after=token)
    gains["b"] = [own, lax.ppermute(give, "xl", [(0, 1), (1, 0)])]
    token = second_early("b", second_early("a", token))
    grad_here, token = late(grad_here, token)
    back = lax.all_to_all(
        grad_here.reshape(8, 4, 8, D), ("z", "xl"), split_axis=0, concat_axis=0, tiled=True
    )
    token = second_relay("b", second_relay("a", token))
    token = third("b", third("a", token))
    (total_a,), token = call(add_body, [shape(20, WIDTH_A, F32)], state["a"], after=token)
    grad_tokens, token = pl.pallas_call(
        join_body,
        out_shape=[jax.ShapeDtypeStruct((4, 8, 8, D), BF16), pltpu.VMEM((8, 128), F32)],
        in_specs=[anywhere, in_vmem], out_specs=[anywhere, in_vmem],
        scratch_shapes=[pltpu.SemaphoreType.DMA((4,))], compiler_params=params,
        cost_estimate=pl.CostEstimate(flops=10**7, bytes_accessed=1, transcendentals=0),
    )(back, pltpu.with_memory_space_constraint(token[0], pltpu.VMEM))
    (here, other), token = call(
        final_body, [shape(10, WIDTH_A + WIDTH_B, F32)] * 2, [place, total_a] + state["b"],
        scalars=1, after=[token],
    )
    theirs = swap(other)
    (qkv_grad, out_grad, gain_grad), _ = call(
        assemble_body, [shape(10, 3 * D, F32), shape(10, D, F32), shape(1, 10, F32)],
        [place, here, theirs], scalars=1, results=jax.ShapeDtypeStruct, last=True,
        after=token,
    )
    return (grad_tokens.reshape(1, 4, 64, D), qkv_grad, out_grad, gain_grad.reshape(10))


def solution(mesh):
    fine = Mesh(mesh.devices.reshape(4, 2, 2, 4, 2), ("z", "xl", "xh", "y", "c"))
    tm, space = ("z", "xl"), ("xh", "y", "c")
    tokens = P(None, tm, space, None)
    in_specs = (tokens, tokens, P(), P(), P())
    out_specs = (tokens, P(tm + space, None), P(tm + space, None), P(tm + space))
    return jax.shard_map(
        on_device, mesh=fine, in_specs=in_specs, out_specs=out_specs, check_vma=False
    )
```

```python
import functools
import math

import jax
import jax.numpy as jnp
from jax import lax
from jax.experimental import pallas as pl
from jax.experimental.pallas import tpu as pltpu
from jax.sharding import Mesh, PartitionSpec as P

D = 1280
HEADS = 16
HEAD = 80
HALF = 640
TOKENS = 256
INVERSE_ROOT = 1.0 / math.sqrt(HEAD)
FACTOR = 1.0 / math.sqrt(32 * 1024)
BF16, F32 = jnp.bfloat16, jnp.float32
ORDER_A = (("z", "y", "x"), ("y", "x", "z"))
ORDER_B = (("x", "z", "y"), ("x", "z", "y"))
WIDTH_A, WIDTH_B = 1920, 768
NN = (((1,), (0,)), ((), ()))
NT = (((1,), (1,)), ((), ()))
TN = (((0,), (0,)), ((), ()))


def dot(left, right, dims=NN):
    return lax.dot_general(left, right, dims, preferred_element_type=F32)


def call(body, outs, operands, scalars=0, flops=0, scratch=(), after=None, results=pltpu.VMEM,
         hbm=(), last=False):
    vmem = pl.BlockSpec(memory_space=pltpu.VMEM)
    smem = pl.BlockSpec(memory_space=pltpu.SMEM)
    count, tokens = len(operands), [] if last else [pltpu.VMEM((8, 128), F32)]
    size = sum(math.prod(o.shape) * o.dtype.itemsize for o in list(operands) + list(outs))
    given = list(operands) + ([] if after is None else list(after))
    spaces = [smem] * scalars + [vmem] * (len(given) - scalars)
    placed = [
        value if place < scalars else pltpu.with_memory_space_constraint(value, pltpu.VMEM)
        for place, value in enumerate(given)
    ]
    for place in hbm:
        spaces[place] = pl.BlockSpec(memory_space=pl.ANY)
        placed[place] = from_hbm(given[place])

    def run(*refs):
        results, rest = refs[len(placed):len(placed) + len(outs)], refs[len(placed) + len(outs):]
        if not last:
            rest[0][...] = jnp.zeros((8, 128), F32)
            rest = rest[1:]
        body(*refs[:count], *results, *rest)

    given = pl.pallas_call(
        run,
        out_shape=[results(o.shape, o.dtype) for o in outs] + tokens,
        in_specs=spaces,
        out_specs=[vmem] * (len(outs) + len(tokens)),
        scratch_shapes=scratch,
        compiler_params=pltpu.CompilerParams(vmem_limit_bytes=16 * 2**20),
        cost_estimate=pl.CostEstimate(
            flops=flops, bytes_accessed=size // 4 if flops else 1, transcendentals=0
        ),
    )(*placed)
    return list(given[:len(outs)]), list(given[len(outs):])


def late(value, after):
    vmem, anywhere = pl.BlockSpec(memory_space=pltpu.VMEM), pl.BlockSpec(memory_space=pl.ANY)

    def body(*refs):
        refs[-1][...] = jnp.zeros((8, 128), F32)

    value, token = pl.pallas_call(
        body,
        out_shape=[jax.ShapeDtypeStruct(value.shape, value.dtype), pltpu.VMEM((8, 128), F32)],
        in_specs=[anywhere] + [vmem] * len(after), out_specs=[anywhere, vmem],
        input_output_aliases={0: 0},
        compiler_params=pltpu.CompilerParams(vmem_limit_bytes=2**20),
        cost_estimate=pl.CostEstimate(flops=10**7, bytes_accessed=1, transcendentals=0),
    )(value, *[pltpu.with_memory_space_constraint(array, pltpu.VMEM) for array in after])
    return value, [token]


def from_hbm(value):
    return pltpu.with_memory_space_constraint(value, pltpu.HBM)


def shape(rows, columns, kind=BF16):
    return jax.ShapeDtypeStruct((rows, columns), kind)


def side(both_ref, which, columns=slice(None)):
    value = both_ref[:, 32 * which:32 * which + 32, columns]
    return value.reshape(TOKENS, value.shape[-1])


def normalize(both_ref):
    x_wide = side(both_ref, 0).astype(F32)
    centred = x_wide - jnp.mean(x_wide, axis=-1, keepdims=True)
    variance = jnp.mean(centred * centred, axis=-1, keepdims=True)
    inv_std = lax.rsqrt(variance + 1e-06)
    return centred * inv_std, inv_std


def half(place_ref, own):
    core = place_ref[3] if own else 1 - place_ref[3]
    return pl.ds(pl.multiple_of(core * HALF, 128), HALF)


def forward_body(place_ref, both_ref, gain_ref, weight_ref, out_weight_ref, gained_ref, qkv_ref, cot_ref,
                 held_ref, hat_ref, inv_ref, out_held_ref, sems):
    pieces = [slice(step * HALF, (step + 1) * HALF) for step in range(6)]
    copies = [
        pltpu.make_async_copy(weight_ref.at[:, piece], held_ref.at[:, piece], sems.at[step])
        for step, piece in enumerate(pieces)
    ]
    copies.append(pltpu.make_async_copy(out_weight_ref, out_held_ref, sems.at[6]))
    for copy in copies[:3]:
        copy.start()
    normalized, inv_std = normalize(both_ref)
    hat_ref[...] = normalized
    inv_ref[...] = jnp.broadcast_to(inv_std, (TOKENS, 128))
    gained = (normalized * gain_ref[...]).astype(BF16)
    gained_ref[...] = gained
    cot_ref[...] = side(both_ref, 1, half(place_ref, False))
    for step, (copy, piece) in enumerate(zip(copies, pieces)):
        copy.wait()
        if step + 3 < len(copies):
            copies[step + 3].start()
        qkv_ref[:, piece] = dot(gained, held_ref[:, piece]).astype(BF16)
    copies[6].wait()


def attention_body(group_ref, qkv_ref, both_ref, weight_ref, att_ref, stack_ref, ag_ref,
                   bias_ref):
    start = pl.multiple_of(group_ref[0] * HALF, 128)
    ag_ref[...] = dot(side(both_ref, 1), weight_ref[pl.ds(start, HALF), :], NT).astype(BF16)
    row = lax.broadcasted_iota(jnp.int32, (TOKENS, TOKENS), 0)
    column = lax.broadcasted_iota(jnp.int32, (TOKENS, TOKENS), 1)
    bias_ref[...] = jnp.where((row & 7) == (column & 7), 0.0, -1e30)
    tiles = [[[] for _ in range(5)] for _ in range(4)]
    for head in range(8):
        low, high = head * HEAD, (head + 1) * HEAD
        first, last = low // 128 * 128, -(-high // 128) * 128
        width = last - first
        lanes = lax.broadcasted_iota(jnp.int32, (1, width), 1) + first
        keep = jnp.where((lanes >= low) & (lanes < high), 1.0, 0.0).astype(BF16)

        def cut(part):
            return qkv_ref[:, pl.ds(pl.multiple_of(start + part * D + first, 128), width)] * keep

        query, key, value = cut(0), cut(1), cut(2)
        grad = ag_ref[:, first:last] * keep
        scores = dot(key, query, NT) + bias_ref[...]
        shifted = jnp.exp((scores - jnp.max(scores, axis=0, keepdims=True)) * INVERSE_ROOT)
        prob = shifted * (1.0 / jnp.sum(shifted, axis=0, keepdims=True))
        prob_low = prob.astype(BF16)
        prob_grad = dot(value, grad, NT)
        mixed = jnp.sum(prob_grad * prob, axis=0, keepdims=True)
        score_grad = (prob * (prob_grad - mixed) * INVERSE_ROOT).astype(BF16)
        results = (
            dot(prob_low, value, TN), dot(score_grad, key, TN), dot(score_grad, query),
            dot(prob_low, grad),
        )
        for kind, result in enumerate(results):
            for tile in range(width // 128):
                piece = result[:, tile * 128:(tile + 1) * 128]
                tiles[kind][first // 128 + tile].append(piece)
    for kind in range(4):
        for tile in range(5):
            total = sum(tiles[kind][tile][1:], tiles[kind][tile][0]).astype(BF16)
            if kind == 0:
                att_ref[:, tile * 128:(tile + 1) * 128] = total
            else:
                at = (kind - 1) * HALF + tile * 128
                stack_ref[:, at:at + 128] = total


def joint_attention_body(group_ref, qkv_ref, both_ref, weight_ref, out_ref, *scratch):
    attention_body(
        group_ref, qkv_ref, both_ref, weight_ref, out_ref.at[:, :HALF], out_ref.at[:, HALF:],
        *scratch
    )


def input_grad_body(place_ref, both_ref, hat_ref, inv_ref, gain_ref, weight_ref, mine_ref,
                    other_ref, pick_ref,
                    grad_ref, keep, give, joined_ref):
    for own, stack_ref in ((True, mine_ref), (False, other_ref)):
        group = place_ref[3] if own else 1 - place_ref[3]
        for part in range(3):
            columns = pl.ds(pl.multiple_of(group * HALF + part * D, 128), HALF)
            start = part * HALF if own else (part + 1) * HALF
            joined_ref[:, columns] = stack_ref[:, start:start + HALF]
    normed_grad = dot(joined_ref[...], weight_ref[...], NT)
    normalized, inv_std = hat_ref[...], inv_ref[:, 0:1]
    scaled = normed_grad * gain_ref[...]
    inner = scaled - jnp.mean(scaled, axis=-1, keepdims=True)
    inner -= normalized * jnp.mean(scaled * normalized, axis=-1, keepdims=True)
    grad_ref[...] = (side(both_ref, 1).astype(F32) + inv_std * inner).astype(BF16)
    gain = jnp.sum(normed_grad * normalized, axis=0, keepdims=True)
    high = gain.astype(BF16).astype(F32)
    middle = (gain - high).astype(BF16).astype(F32)
    row = lax.broadcasted_iota(jnp.int32, (16, D), 0)
    split = jnp.where(row == 2, gain - high - middle, 0.0)
    split = jnp.where(row == 0, high, jnp.where(row == 1, middle, split)).astype(BF16)
    blocks = []
    for block in range(4):
        rows = slice(block * 320, (block + 1) * 320)
        ordered = jnp.sum(dot(split, pick_ref[rows, :], NT), axis=0, keepdims=True)
        blocks.append(jnp.concatenate([ordered, jnp.zeros((1, 64), F32)], axis=1))
    even = (place_ref[1] & 1) == 0
    near = jnp.where(even, blocks[1], blocks[3])
    far = jnp.where(even, blocks[3], blocks[1])
    rest = jnp.zeros((6, 384), F32)
    keep[...] = jnp.concatenate([blocks[0], near, rest], axis=0)
    give[...] = jnp.concatenate([blocks[2], far, rest], axis=0)


def gain_body(keep, arrived, own, give):
    total = keep[...] + arrived[...]
    own[...] = total
    give[...] = jnp.concatenate([total[1:8], total[0:1]], axis=0)


def pick(source):
    lanes = lax.broadcasted_iota(jnp.int32, (source.shape[0], D), 1)
    return jnp.where(lanes == source, 1.0, 0.0).astype(BF16)


def relative_rows(place_ref, order, block):
    here = {"z": place_ref[0], "x": place_ref[1], "y": place_ref[2]}
    on_first = place_ref[3] == 0
    row = lax.broadcasted_iota(jnp.int32, (320, 1), 0)

    def count(value, size):
        return sum(jnp.where(value >= size * step, 1, 0) for step in (1, 2, 3))

    def offset(axis, at):
        if axis == "x":
            return (at & 1) * 160 + (at >> 1) * 80
        return at * (320 if axis == "z" else 20)

    second = count(row, 80)
    row = row - 80 * second
    third = count(row, 20)
    row = row - 20 * third
    for level, step in enumerate((block, second, third)):
        one, two = (
            offset(axes[level], (here[axes[level]] + step) & 3) for axes in order
        )
        row = row + jnp.where(on_first, one, two)
    return row


def ready_body(place_ref, pick_a, pick_b, pick_att, token):
    token[...] = jnp.zeros((8, 128), F32)
    for step in range(4):
        rows = slice(step * 320, (step + 1) * 320)
        pick_a[rows, :] = pick(relative_rows(place_ref, ORDER_A, step))
        feature = relative_rows(place_ref, ORDER_B, step)
        pick_b[rows, :] = pick(feature)
        feature = feature + place_ref[3] * HALF
        pick_att[rows, :] = pick(jnp.where(feature >= D, feature - D, feature))


def gained_body(pick_ref, own_ref, partner_ref, out):
    for step in range(4):
        rows = slice(step * 320, (step + 1) * 320)
        out[rows, :TOKENS] = dot(pick_ref[rows, :], own_ref[...], NT).astype(BF16)
        out[rows, TOKENS:] = dot(pick_ref[rows, :], partner_ref[...], NT).astype(BF16)


def turn_body(pick_att, mine, other, their_mine, theirs, att_out):
    sides = ((mine, other), (theirs, their_mine))
    for step in range(4):
        rows = slice(step * 320, (step + 1) * 320)
        for which, (first, second) in enumerate(sides):
            turned = dot(pick_att[rows, :HALF], first[:, :HALF], NT)
            turned += dot(pick_att[rows, HALF:], second[:, :HALF], NT)
            att_out[rows, which * TOKENS:(which + 1) * TOKENS] = turned.astype(BF16)


def term_a(rows, gained, stack, theirs):
    return dot(gained[rows, :TOKENS], stack[...]) + dot(gained[rows, TOKENS:], theirs[:, HALF:])


def term_b(rows, place_ref, both, their_cot, att):
    outer = dot(att[rows, :TOKENS], side(both, 1, half(place_ref, True)))
    return outer + dot(att[rows, TOKENS:], their_cot[...])


def early_body(term, count, *refs):
    plus, minus = refs[count:]
    far = term(slice(640, 960), *refs[:count])
    plus[0:160, :] = far[0:160].astype(BF16)
    minus[0:160, :] = far[160:320].astype(BF16)
    plus[160:320, :] = term(slice(480, 640), *refs[:count]).astype(BF16)
    minus[160:320, :] = term(slice(960, 1120), *refs[:count]).astype(BF16)


def relay_body(term, count, *refs):
    from_minus, from_plus, plus, minus = refs[count:]
    up = term(slice(320, 480), *refs[:count]) + from_minus[0:160, :].astype(F32)
    down = term(slice(1120, 1280), *refs[:count]) + from_plus[0:160, :].astype(F32)
    plus[...] = up.astype(BF16)
    minus[...] = down.astype(BF16)


def own_body(term, count, *refs):
    from_minus, from_plus, own = refs[count:]
    total = term(slice(0, 320), *refs[:count])
    own[0:160, :] = total[0:160] + from_plus[160:320, :].astype(F32)
    own[160:320, :] = total[160:320] + from_minus[160:320, :].astype(F32)


def second_early_body(own, from_minus, from_plus, *refs):
    gains, (rest, plus, minus) = refs[:-3], refs[-3:]
    upper = own[0:160, :] + from_minus[...].astype(F32)
    lower = own[160:320, :] + from_plus[...].astype(F32)
    if gains:
        line = gains[0][0:1, :] + gains[1][0:1, :]
        row = lax.broadcasted_iota(jnp.int32, (320, 384), 0)
        lane = lax.broadcasted_iota(jnp.int32, (320, 384), 1)
        column = jnp.sum(jnp.where(row == lane, line, 0.0), axis=-1, keepdims=True)
        column = jnp.where(lane[:, :128] == 0, column, 0.0)
        upper = jnp.concatenate([upper, column[0:160]], axis=1)
        lower = jnp.concatenate([lower, column[160:320]], axis=1)
    rest[0:120, :] = upper[0:120]
    plus[40:80, :] = upper[120:160]
    plus[0:40, :] = lower[0:40]
    minus[0:80, :] = lower[40:120]
    rest[120:160, :] = lower[120:160]


def second_relay_body(rest, from_minus, from_plus, plus, minus, part):
    plus[...] = rest[80:120, :] + from_minus[0:40, :]
    minus[...] = rest[120:160, :] + from_plus[0:40, :]
    part[0:40, :] = rest[0:40, :] + from_plus[40:80, :]
    part[40:80, :] = rest[40:80, :] + from_minus[40:80, :]


def third_body(part, last_minus, last_plus, own, one, two, three):
    upper = part[0:40, :] + last_minus[...]
    lower = part[40:80, :] + last_plus[...]
    own[...] = upper[0:20]
    one[...] = upper[20:40]
    two[...] = lower[0:20]
    three[...] = lower[20:40]


def add_body(own, one, two, three, out):
    out[...] = (own[...] + one[...]) + (two[...] + three[...])


def final_body(place_ref, total_a, own, one, two, three, here, other):
    on_first = place_ref[3] == 0
    total_b = (own[...] + one[...]) + (two[...] + three[...])
    total = jnp.concatenate([total_a[...], total_b], axis=1)
    low, high = total[0:10], total[10:20]
    here[...] = jnp.where(on_first, low, high)
    other[...] = jnp.where(on_first, high, low)


def assemble_body(place_ref, here, theirs, qkv_ref, out_ref, gain_ref):
    first = place_ref[3] == 0
    left = jnp.where(first, here[...], theirs[...]) * FACTOR
    right = jnp.where(first, theirs[...], here[...]) * FACTOR
    for which, value in enumerate((left, right)):
        out_ref[:, which * HALF:(which + 1) * HALF] = value[:, WIDTH_A:WIDTH_A + HALF]
        for part in range(3):
            at = part * D + which * HALF
            qkv_ref[:, at:at + HALF] = value[:, part * HALF:(part + 1) * HALF]
    both = left[:, WIDTH_A + HALF:] + right[:, WIDTH_A + HALF:]
    column = jnp.sum(both, axis=-1, keepdims=True)
    row = lax.broadcasted_iota(jnp.int32, (10, 10), 0)
    lane = lax.broadcasted_iota(jnp.int32, (10, 10), 1)
    gain_ref[...] = jnp.sum(jnp.where(row == lane, column, 0.0), axis=0, keepdims=True)


def send(value, order, level, step):
    pairs = []
    for source in range(128):
        spots = {
            "z": source // 32, "x": source // 16 % 2 + source // 8 % 2 * 2, "y": source // 2 % 4
        }
        axis = order[source % 2][level]
        spots[axis] = (spots[axis] + step) % 4
        column = spots["x"] % 2 * 2 + spots["x"] // 2
        target = ((spots["z"] * 4 + column) * 4 + spots["y"]) * 2 + source % 2
        pairs.append((source, target))
    return lax.ppermute(value, ("z", "xl", "xh", "y", "c"), pairs)


def swap(value):
    return lax.ppermute(value, "c", [(0, 1), (1, 0)])


def split_body(x_ref, cot_ref, out_ref, sems):
    copies = [
        pltpu.make_async_copy(value.at[frame], out_ref.at[:, which, frame], sems.at[which, frame])
        for which, value in enumerate((x_ref, cot_ref))
        for frame in range(4)
    ]
    for copy in copies:
        copy.start()
    for copy in copies:
        copy.wait()


def join_body(value_ref, after_ref, out_ref, token_ref, sems):
    copies = [
        pltpu.make_async_copy(value_ref.at[:, frame], out_ref.at[frame], sems.at[frame])
        for frame in range(4)
    ]
    for copy in copies:
        copy.start()
    token_ref[...] = after_ref[...]
    for copy in copies:
        copy.wait()


def on_device(activations, grad_out, norm_gain, qkv_weight, out_weight):
    anywhere = pl.BlockSpec(memory_space=pl.ANY)
    in_vmem = pl.BlockSpec(memory_space=pltpu.VMEM)
    params = pltpu.CompilerParams(vmem_limit_bytes=16 * 2**20)
    x_place = lax.axis_index("xh") * 2 + lax.axis_index("xl")
    place = jnp.stack([lax.axis_index("z"), x_place, lax.axis_index("y"), lax.axis_index("c")])
    place = place.astype(jnp.int32)
    group = place[3:]
    gain_row = norm_gain.reshape(1, D)
    both = pl.pallas_call(
        split_body, out_shape=pltpu.VMEM((8, 2, 4, 8, D), BF16), in_specs=[anywhere] * 2,
        out_specs=in_vmem, scratch_shapes=[pltpu.SemaphoreType.DMA((2, 4))],
        compiler_params=params,
    )(from_hbm(activations.reshape(4, 8, 8, D)), from_hbm(grad_out.reshape(4, 8, 8, D)))
    pick_a, pick_b, pick_att, token = pl.pallas_call(
        ready_body, out_shape=[pltpu.HBM((D, D), BF16)] * 3 + [shape(8, 128, F32)],
        in_specs=[pl.BlockSpec(memory_space=pltpu.SMEM)], out_specs=[in_vmem] * 4,
        compiler_params=params,
        cost_estimate=pl.CostEstimate(flops=10**9, bytes_accessed=2 * 10**7, transcendentals=0),
    )(place)
    both = lax.all_to_all(both, ("z", "xl"), split_axis=0, concat_axis=0, tiled=True)
    both = both.reshape(8, 64, D)
    (gained, qkv, cot_other, weight, hat, inv_std, held_out), token = call(
        forward_body,
        [shape(TOKENS, D), shape(TOKENS, 3 * D), shape(TOKENS, HALF), shape(D, 3 * D),
         shape(TOKENS, D, F32), shape(TOKENS, 128, F32), shape(D, D)],
        [place, both, gain_row, qkv_weight, out_weight], scalars=1, flops=2 * TOKENS * D * 3 * D,
        scratch=[pltpu.SemaphoreType.DMA((7,))], hbm=(3, 4), after=[token],
    )
    their_gained, their_cot = swap(gained), swap(cot_other)

    def attention(which, after, outs):
        return call(
            attention_body if len(outs) == 2 else joint_attention_body, outs,
            [which, qkv, both, held_out], scalars=1, flops=5 * 10**9,
            scratch=[pltpu.VMEM((TOKENS, HALF), BF16), pltpu.VMEM((TOKENS, TOKENS), F32)],
            after=after,
        )

    (other_half,), token = attention(1 - group, token, [shape(TOKENS, 4 * HALF)])
    their_half = swap(other_half)
    (att_mine, stack), token = attention(
        group, token, [shape(TOKENS, HALF), shape(TOKENS, 3 * HALF)]
    )
    their_mine = swap(att_mine)
    (gained_a,), token = call(
        gained_body, [shape(D, 512)], [pick_a, gained, their_gained], flops=2 * D * D * 512,
        after=token,
    )
    work = {"a": 10**7, "b": 15 * 10**8, "b second": 8 * 10**9}
    base = {"a": [gained_a, stack, their_half]}
    kinds = {"a": (term_a, 0, WIDTH_A, ORDER_A), "b": (term_b, 1, HALF, ORDER_B)}

    def run(which, body, outs, extra, after):
        term, scalars, _, _ = kinds[which]
        return call(
            functools.partial(body, term, len(base[which])), outs, base[which] + extra,
            scalars=scalars, flops=work[which], after=after,
        )

    def exchange(which, sent, level):
        order = kinds[which][3]
        return [send(sent[0], order, level, 1), send(sent[1], order, level, 3)]

    state = {}

    def early(which, after):
        sent, after = run(which, early_body, [shape(320, kinds[which][2])] * 2, [], after)
        state[which] = exchange(which, sent, 0)
        return after

    def relay(which, after):
        width, first = kinds[which][2], state[which]
        sent, after = run(which, relay_body, [shape(160, width)] * 2, first, after)
        state[which] = (first, exchange(which, sent, 0))
        return after

    def own_rows(which, after):
        first, second = state[which]
        outs = [shape(320, kinds[which][2], F32)]
        own, after = run(which, own_body, outs, first, after)
        state[which] = own + second
        return after

    gains = {"a": [], "b": []}

    def second_early(which, after):
        width = kinds[which][2] + (128 if gains[which] else 0)
        outs = [shape(rows, width, F32) for rows in (160, 80, 80)]
        (rest, *sent), after = call(
            second_early_body, outs, state[which] + gains[which], after=after,
            flops=work["b second" if which == "b" else "a"],
        )
        state[which] = [rest] + exchange(which, sent, 1)
        return after

    def second_relay(which, after):
        width = state[which][0].shape[1]
        outs = [shape(40, width, F32)] * 2 + [shape(80, width, F32)]
        (plus, minus, part), after = call(
            second_relay_body, outs, state[which], flops=work[which], after=after
        )
        state[which] = [part] + exchange(which, (plus, minus), 1)
        return after

    def third(which, after):
        outs = [shape(20, state[which][0].shape[1], F32)] * 4
        (own, *others), after = call(
            third_body, outs, state[which], flops=work[which], after=after
        )
        order = kinds[which][3]
        sent = [send(other, order, 2, step + 1) for step, other in enumerate(others)]
        state[which] = [own] + sent
        return after

    token = early("a", token + [their_mine])
    (att,), token = call(
        turn_body, [shape(D, 512)], [pick_att, att_mine, other_half, their_mine, their_half],
        after=token,
    )
    base["b"] = [place, both, their_cot, att]
    token = early("b", token)
    (grad_here, keep, give), token = call(
        input_grad_body, [shape(TOKENS, D)] + [shape(8, 384, F32)] * 2,
        [place, both, hat, inv_std, gain_row, weight, stack, other_half, pick_b], scalars=1,
        after=token,
        scratch=[pltpu.VMEM((TOKENS, 3 * D), BF16)],
    )
    arrived = lax.ppermute(give, "xh", [(0, 1), (1, 0)])
    token = relay("b", relay("a", token))
    token = own_rows("b", own_rows("a", token))
    (own, give), token = call(gain_body, [shape(8, 384, F32)] * 2, [keep, arrived], after=token)
    gains["b"] = [own, lax.ppermute(give, "xl", [(0, 1), (1, 0)])]
    token = second_early("b", second_early("a", token))
    grad_here, token = late(grad_here, token)
    back = lax.all_to_all(
        grad_here.reshape(8, 4, 8, D), ("z", "xl"), split_axis=0, concat_axis=0, tiled=True
    )
    token = second_relay("b", second_relay("a", token))
    token = third("b", third("a", token))
    (total_a,), token = call(add_body, [shape(20, WIDTH_A, F32)], state["a"], after=token)
    grad_tokens, token = pl.pallas_call(
        join_body,
        out_shape=[jax.ShapeDtypeStruct((4, 8, 8, D), BF16), pltpu.VMEM((8, 128), F32)],
        in_specs=[anywhere, in_vmem], out_specs=[anywhere, in_vmem],
        scratch_shapes=[pltpu.SemaphoreType.DMA((4,))], compiler_params=params,
        cost_estimate=pl.CostEstimate(flops=10**7, bytes_accessed=1, transcendentals=0),
    )(back, pltpu.with_memory_space_constraint(token[0], pltpu.VMEM))
    (here, other), token = call(
        final_body, [shape(10, WIDTH_A + WIDTH_B, F32)] * 2, [place, total_a] + state["b"],
        scalars=1, after=[token],
    )
    theirs = swap(other)
    (qkv_grad, out_grad, gain_grad), _ = call(
        assemble_body, [shape(10, 3 * D, F32), shape(10, D, F32), shape(1, 10, F32)],
        [place, here, theirs], scalars=1, results=jax.ShapeDtypeStruct, last=True,
        after=token,
    )
    return (grad_tokens.reshape(1, 4, 64, D), qkv_grad, out_grad, gain_grad.reshape(10))


def solution(mesh):
    fine = Mesh(mesh.devices.reshape(4, 2, 2, 4, 2), ("z", "xl", "xh", "y", "c"))
    tm, space = ("z", "xl"), ("xh", "y", "c")
    tokens = P(None, tm, space, None)
    in_specs = (tokens, tokens, P(), P(), P())
    out_specs = (tokens, P(tm + space, None), P(tm + space, None), P(tm + space))
    return jax.shard_map(
        on_device, mesh=fine, in_specs=in_specs, out_specs=out_specs, check_vma=False
    )
```
